32 devices in a mesh: groups: 2 (over x), row: 16 (over z, y, core).
Axes of the slice: x: 2, y: 2, z: 4, core: 2. Of those that a mesh axis runs over, the one named last changes fastest.
Arguments:
- homolog_features: bfloat16 [64, 512, 256], P(None, ('groups', 'row')), parts along dimension 1, may hold values from -6 to 6
- coverage_indicator: int32 [64, 512], P(None, ('groups', 'row')), parts along dimension 1, may hold values from 0 to 1, as said below
- couple_features: bfloat16 [512, 256, 128], P(('groups', 'row')), parts along dimension 0, may hold values from -6 to 6
- observed_indicator: int32 [512], P('groups'), parts along dimension 0, may hold values 0 or 1
- first_factor_matrix: bfloat16 [256, 32], replicated, may hold values from -0.375 to 0.375
- second_factor_matrix: bfloat16 [256, 32], replicated, may hold values from -0.375 to 0.375
- product_final_matrix: bfloat16 [1024, 128], replicated, may hold values from -0.5 to 0.5
- edge_projection_matrix: bfloat16 [128, 512], replicated, may hold values from -0.5 to 0.5
- sigmoid_filter_matrix: bfloat16 [128, 128], replicated, may hold values from -0.5 to 0.5
- multiplicative_final_matrix: bfloat16 [128, 128], replicated, may hold values from -0.5 to 0.5
Outputs:
- new_pair: bfloat16 [512, 256, 128], P(('groups', 'row')), parts along dimension 0
The draws below stay inside these ranges and needn't reach their ends.
There are 2 independent parts, one for each index of `groups`. The reference program is written for one: setup_inputs(seed, part) draws one part's arguments, and reference() takes and returns one part's arrays. A program takes and returns all parts, laid end to end along the dimension named above; an argument that names none is the same for every part. Nothing has to cross between parts.
Inputs may be any that keep to these rules, and one draw needn't show every extreme that they name: `coverage_indicator`: each residue is covered by a leading run of sequences whose depth varies by residue, with gaps inside it; some residues have depth zero.
All inputs are finite; a program needn't handle non-finite values.
Results may differ from the reference program's by a relative error of at most 0.0064.
Values may be sent and summed in bfloat16 or wider, within the bound.
No kernel may reach another device: no remote copies, remote signals or barrier semaphores. Data moves between devices by JAX's collectives and lax.ppermute only.
A program may use at most 128 MiB of HBM per device.

```python
import jax
import jax.numpy as jnp
from jax import lax

FEATURE_BREADTH = 256
C = 128
REDUCED_DIM = 32
HID = 128
HOMOLOG_NUMBER = 64
RES_DEV = 16
CHAIN_LENGTH = 256
N_ROW = 16


def draw_coverage_indicator(key, part):
    key = jax.random.fold_in(key, 11)
    depth_key, gap_key = jax.random.split(key)
    depth = jnp.maximum(jax.random.randint(depth_key, (CHAIN_LENGTH,), -(HOMOLOG_NUMBER // 4), HOMOLOG_NUMBER + 1), 0)
    gaps = jax.random.randint(gap_key, (HOMOLOG_NUMBER, CHAIN_LENGTH), 0, 4) > 0
    seq_index = jnp.arange(HOMOLOG_NUMBER, dtype=jnp.int32)[:, None]
    covered = seq_index < depth[None, :]
    return (covered & gaps).astype(jnp.int32)


def place_ends(drawn, rng, least, largest):
    place = [jax.random.randint(jax.random.fold_in(rng, axis), (), 0, length) for axis, length in enumerate(drawn.shape)]
    main_axis = drawn.shape.index(max(drawn.shape))
    next_to = place[:main_axis] + [(place[main_axis] + 1) % drawn.shape[main_axis]] + place[main_axis + 1:]
    return drawn.at[tuple(place)].set(least).at[tuple(next_to)].set(largest)


def level_of(key, dims, cuts, least, high):
    level = 1.0
    for dim, parts in cuts:
        steps = jax.random.uniform(jax.random.fold_in(jax.random.fold_in(key, 6), dim), (parts,), jnp.float32, least / len(cuts), high / len(cuts))
        level = level * jnp.repeat(jnp.exp(steps), dims[dim] // parts).reshape((-1,) + (1,) * (len(dims) - 1 - dim))
    return level


def noise(key, dims, scale, reach, cuts=(), kind=jnp.bfloat16):
    values = jax.random.normal(key, dims, jnp.float32) * scale
    if len(cuts) > 0:
        values = level_of(key, dims, cuts, -0.22, 0.18) * values
    return jnp.clip(values, min=-reach, max=reach).astype(kind)


def setup_inputs(seed: int = 0, part: int = 0) -> dict:
    key_list = jax.random.split(jax.random.key(seed), 11)
    part_splits = jax.random.split(jax.random.fold_in(key_list[10], part), 11)
    homolog_features = noise(part_splits[0], (HOMOLOG_NUMBER, CHAIN_LENGTH, FEATURE_BREADTH), 1.0, 6.0, ((1, 16),))
    coverage_indicator = draw_coverage_indicator(jax.random.fold_in(jax.random.fold_in(key_list[10], part), 71), part)
    couple_features = noise(part_splits[2], (CHAIN_LENGTH, CHAIN_LENGTH, C), 1.0, 6.0, ((0, 16),))
    observed_indicator = place_ends((jax.random.randint(part_splits[3], (CHAIN_LENGTH,), 0, 8) < 7).astype(jnp.int32), jax.random.fold_in(part_splits[3], 1), 0, 1)
    first_factor_matrix = noise(key_list[4], (FEATURE_BREADTH, REDUCED_DIM), FEATURE_BREADTH ** -0.5, 0.375)
    second_factor_matrix = noise(key_list[5], (FEATURE_BREADTH, REDUCED_DIM), FEATURE_BREADTH ** -0.5, 0.375)
    product_final_matrix = noise(key_list[6], (REDUCED_DIM * REDUCED_DIM, C), (REDUCED_DIM * REDUCED_DIM // 8) ** -0.5, 0.5)
    edge_projection_matrix = noise(key_list[7], (C, 4 * HID), C ** -0.5, 0.5)
    sigmoid_filter_matrix = noise(key_list[8], (C, C), C ** -0.5, 0.5)
    multiplicative_final_matrix = noise(key_list[9], (HID, C), HID ** -0.5, 0.5)
    return dict(homolog_features=homolog_features, coverage_indicator=coverage_indicator, couple_features=couple_features, observed_indicator=observed_indicator, first_factor_matrix=first_factor_matrix, second_factor_matrix=second_factor_matrix, product_final_matrix=product_final_matrix, edge_projection_matrix=edge_projection_matrix, sigmoid_filter_matrix=sigmoid_filter_matrix, multiplicative_final_matrix=multiplicative_final_matrix)


def standardize_module(value):
    mean = lax.optimization_barrier(jnp.mean(value, axis=-1, keepdims=True))
    centred = value - mean
    var = lax.optimization_barrier(jnp.mean(centred * centred, axis=-1, keepdims=True))
    return centred * lax.rsqrt(var + 1e-05)

def reference(homolog_features, coverage_indicator, couple_features, observed_indicator, first_factor_matrix, second_factor_matrix, product_final_matrix, edge_projection_matrix, sigmoid_filter_matrix, multiplicative_final_matrix):
    float_thirty_two = jnp.float32
    mask_values = coverage_indicator.astype(float_thirty_two)
    homolog_standardizer = standardize_module(homolog_features.astype(float_thirty_two)).astype(jnp.bfloat16).astype(float_thirty_two)
    left_side = (jnp.einsum('hnl,lm->hnm', homolog_standardizer, first_factor_matrix.astype(float_thirty_two)) * mask_values[..., None]).astype(jnp.bfloat16)
    right_side = (jnp.einsum('hnl,lm->hnm', homolog_standardizer, second_factor_matrix.astype(float_thirty_two)) * mask_values[..., None]).astype(jnp.bfloat16)
    mask_bfloat = coverage_indicator.astype(jnp.bfloat16)
    count = jnp.dot(mask_bfloat.T, mask_bfloat, preferred_element_type=float_thirty_two)
    left_blocks = left_side.reshape(HOMOLOG_NUMBER, N_ROW, RES_DEV, REDUCED_DIM).transpose(1, 0, 2, 3)
    count_blocks = count.reshape(N_ROW, RES_DEV, CHAIN_LENGTH)
    right32 = right_side.astype(float_thirty_two)
    w_out32 = product_final_matrix.astype(float_thirty_two)

    def one_block(items):
        block_left, block_count = items
        outer = jnp.einsum('sip,sjq->ijpq', block_left.astype(float_thirty_two), right32).astype(jnp.bfloat16)
        outer = outer.reshape(RES_DEV, CHAIN_LENGTH, REDUCED_DIM * REDUCED_DIM).astype(float_thirty_two)
        update = jnp.einsum('ijf,fc->ijc', outer, w_out32)
        return update / jnp.maximum(block_count, 1.0)[..., None]
    update = lax.map(one_block, (left_blocks, count_blocks)).reshape(CHAIN_LENGTH, CHAIN_LENGTH, C)
    pair_one = couple_features.astype(float_thirty_two) + update
    pair_norm = standardize_module(pair_one).astype(jnp.bfloat16).astype(float_thirty_two)
    w_in32 = edge_projection_matrix.astype(float_thirty_two)
    resid = observed_indicator.astype(float_thirty_two)
    pair_mask = (resid[:, None] * resid[None, :])[..., None]

    def side(offset):
        gate_part = jnp.einsum('ijc,cd->ijd', pair_norm, w_in32[:, offset:offset + HID])
        value_part = jnp.einsum('ijc,cd->ijd', pair_norm, w_in32[:, offset + HID:offset + 2 * HID])
        return (jax.nn.sigmoid(gate_part) * value_part * pair_mask).astype(jnp.bfloat16)
    side_a = side(0)
    side_b = side(2 * HID)
    tri = jnp.einsum('ikc,jkc->ijc', side_a.astype(float_thirty_two), side_b.astype(float_thirty_two)).astype(jnp.bfloat16)
    tri_norm = standardize_module(tri.astype(float_thirty_two)).astype(jnp.bfloat16).astype(float_thirty_two)
    gate = jax.nn.sigmoid(jnp.einsum('ijc,cd->ijd', pair_norm, sigmoid_filter_matrix.astype(float_thirty_two)))
    result = pair_one + gate * jnp.einsum('ijh,hc->ijc', tri_norm, multiplicative_final_matrix.astype(float_thirty_two))
    return result.astype(jnp.bfloat16)
```

```python
import jax
import jax.numpy as jnp
from jax import lax
from jax.experimental import pallas as pl
from jax.experimental.pallas import tpu as pltpu
from jax.sharding import PartitionSpec as P

F32 = jnp.float32
BF16 = jnp.bfloat16
LANES = 128
NT = (((1,), (1,)), ((), ()))
VMEM_LIMIT = 56 * 1024 * 1024


def params(steps=1):
    return pltpu.CompilerParams(
        vmem_limit_bytes=VMEM_LIMIT, dimension_semantics=("arbitrary",) * steps
    )


def sigmoid(value):
    return 0.5 * jnp.tanh(0.5 * value) + 0.5


def standardize(value, axis):
    mean = jnp.mean(value, axis=axis, keepdims=True)
    centred = value - mean
    var = jnp.mean(centred * centred, axis=axis, keepdims=True)
    return centred * lax.rsqrt(var + 1e-05)


def pair_kernel(
    left_ref, right_ref, mask_ref, couple_ref, w_out_ref, w_in_ref, obs_ref,
    pair_ref, norm_ref, a_ref, b_ref, outer, scratch_a, scratch_b,
):
    rows, block, width = couple_ref.shape
    hidden = a_ref.shape[0]
    tiles = block // LANES
    pairs = right_ref.shape[1] - 1
    proj = w_out_ref.shape[1] // (2 * pairs)

    def right_slice(index):
        return right_ref[:, pl.ds(index, 1)].reshape(block, LANES)

    @pl.loop(0, pairs)
    def _(t):
        both = lax.dot_general(
            left_ref[...], right_slice(t), NT, preferred_element_type=F32
        ).astype(BF16)
        half = rows * proj
        for e in range(2):
            outer[:, pl.ds(pl.multiple_of((2 * t + e) * proj, proj), proj), :] = both[
                e * half : (e + 1) * half
            ].reshape(rows, proj, block)

    count = lax.dot_general(mask_ref[...], right_slice(pairs), NT, preferred_element_type=F32)
    scale = 1.0 / jnp.maximum(count, 1.0)

    for i in range(rows):
        update = jnp.dot(w_out_ref[...], outer[i], preferred_element_type=F32)
        pair = couple_ref[i].astype(F32).T + update * scale[i : i + 1]
        pair_ref[i] = pair
        norm = standardize(pair, 0).astype(BF16)
        norm_ref[i] = norm
        sides = jnp.dot(w_in_ref[...], norm, preferred_element_type=F32)
        seen = obs_ref[i : i + 1]
        side_a = sigmoid(sides[:hidden]) * sides[hidden : 2 * hidden] * seen
        side_b = sigmoid(sides[2 * hidden : 3 * hidden]) * sides[3 * hidden :] * seen
        for tile in range(tiles):
            cols = slice(tile * LANES, (tile + 1) * LANES)
            scratch_a[tile, i * hidden : (i + 1) * hidden] = side_a[:, cols]
            scratch_b[tile, i * hidden : (i + 1) * hidden] = side_b[:, cols]

    @pl.loop(0, hidden, unroll=8)
    def _(d):
        for tile in range(tiles):
            cols = slice(tile * LANES, (tile + 1) * LANES)
            a_ref[d, :, cols] = scratch_a[tile, pl.ds(d, rows, stride=hidden), :].astype(BF16)
            b_ref[d, :, cols] = scratch_b[tile, pl.ds(d, rows, stride=hidden), :].astype(BF16)


def pair_stage(left, right, mask, couple, w_out, w_in, obs):
    rows, total, width = couple.shape
    block = 2 * LANES
    devs = block // rows
    hidden = w_in.shape[0] // 4
    return pl.pallas_call(
        pair_kernel,
        grid=(total // block,),
        in_specs=[
            pl.BlockSpec(left.shape, lambda j: (0, 0)),
            pl.BlockSpec((devs,) + right.shape[1:], lambda j: (j, 0, 0, 0)),
            pl.BlockSpec(mask.shape, lambda j: (0, 0)),
            pl.BlockSpec((rows, block, width), lambda j: (0, j, 0)),
            pl.BlockSpec(w_out.shape, lambda j: (0, 0)),
            pl.BlockSpec(w_in.shape, lambda j: (0, 0)),
            pl.BlockSpec((rows, block), lambda j: (0, j)),
        ],
        out_specs=[
            pl.BlockSpec((rows, width, block), lambda j: (0, 0, j)),
            pl.BlockSpec((rows, width, block), lambda j: (0, 0, j)),
            pl.BlockSpec((hidden, rows, block), lambda j: (0, 0, j)),
            pl.BlockSpec((hidden, rows, block), lambda j: (0, 0, j)),
        ],
        out_shape=[
            jax.ShapeDtypeStruct((rows, width, total), F32),
            jax.ShapeDtypeStruct((rows, width, total), BF16),
            jax.ShapeDtypeStruct((hidden, rows, total), BF16),
            jax.ShapeDtypeStruct((hidden, rows, total), BF16),
        ],
        scratch_shapes=[
            pltpu.VMEM((rows, w_out.shape[1], block), BF16),
            pltpu.VMEM((block // LANES, rows * hidden, LANES), F32),
            pltpu.VMEM((block // LANES, rows * hidden, LANES), F32),
        ],
        compiler_params=params(),
        cost_estimate=pl.CostEstimate(
            flops=4 * rows * total * w_out.shape[1] * width,
            bytes_accessed=16 * rows * total * width,
            transcendentals=2 * rows * total * hidden,
        ),
        name="pair_stage",
    )(left, right, mask, couple, w_out, w_in, obs)


def gate_kernel(norm_ref, w_ref, gate_ref):
    for i in range(norm_ref.shape[0]):
        gate_ref[i] = sigmoid(jnp.dot(w_ref[...], norm_ref[i], preferred_element_type=F32))


def gate_stage(norm, weight):
    rows, width, total = norm.shape
    block = 2 * LANES
    spec = pl.BlockSpec((rows, width, block), lambda j: (0, 0, j))
    return pl.pallas_call(
        gate_kernel,
        grid=(total // block,),
        in_specs=[spec, pl.BlockSpec(weight.shape, lambda j: (0, 0))],
        out_specs=spec,
        out_shape=jax.ShapeDtypeStruct((rows, width, total), F32),
        compiler_params=params(),
        cost_estimate=pl.CostEstimate(
            flops=2 * rows * total * width * width,
            bytes_accessed=6 * rows * total * width,
            transcendentals=rows * total * width,
        ),
        name="gate_stage",
    )(norm, weight)


def tri_kernel(a_ref, b_ref, out_ref):
    parts, chans, rows, total = a_ref.shape
    for c in range(chans):
        product = lax.dot_general(
            a_ref[:, c].reshape(parts * rows, total),
            b_ref[:, c].reshape(parts * rows, total),
            NT,
            preferred_element_type=F32,
        )
        out_ref[:, c] = product.astype(BF16).reshape(out_ref.shape[0], rows, -1)


def tri_stage(side_a, side_b):
    parts, chans, rows, total = side_a.shape
    step = max(1, min(chans, chans * 256 // total))
    spec = pl.BlockSpec((parts, step, rows, total), lambda c: (0, c, 0, 0))
    return pl.pallas_call(
        tri_kernel,
        grid=(chans // step,),
        in_specs=[spec, spec],
        out_specs=spec,
        out_shape=jax.ShapeDtypeStruct(side_a.shape, BF16),
        compiler_params=params(),
        cost_estimate=pl.CostEstimate(
            flops=2 * chans * total**3, bytes_accessed=6 * chans * total**2, transcendentals=0
        ),
        name="tri_stage",
    )(side_a, side_b)


def final_kernel(tri_ref, pair_ref, gate_ref, w_ref, out_ref, normed):
    hidden, rows, block = tri_ref.shape
    tiles = block // LANES
    tri = tri_ref[...].astype(F32)
    values = standardize(tri, 0)
    for tile in range(tiles):
        normed[tile] = values[:, :, tile * LANES : (tile + 1) * LANES].reshape(hidden * rows, LANES)
    for i in range(rows):
        columns = jnp.concatenate(
            [normed[tile, pl.ds(i, hidden, stride=rows), :] for tile in range(tiles)], axis=1
        ).astype(BF16)
        update = jnp.dot(w_ref[...], columns, preferred_element_type=F32)
        result = pair_ref[i] + gate_ref[i] * update
        out_ref[i] = result.T.astype(BF16)


def final_stage(tri, pair, gate, weight):
    hidden, rows, total = tri.shape
    width = weight.shape[0]
    block = 2 * LANES
    spec = pl.BlockSpec((rows, width, block), lambda j: (0, 0, j))
    return pl.pallas_call(
        final_kernel,
        grid=(total // block,),
        in_specs=[
            pl.BlockSpec((hidden, rows, block), lambda j: (0, 0, j)),
            spec,
            spec,
            pl.BlockSpec(weight.shape, lambda j: (0, 0)),
        ],
        out_specs=pl.BlockSpec((rows, block, width), lambda j: (0, j, 0)),
        out_shape=jax.ShapeDtypeStruct((rows, total, width), BF16),
        scratch_shapes=[pltpu.VMEM((block // LANES, hidden * rows, LANES), F32)],
        compiler_params=params(),
        cost_estimate=pl.CostEstimate(
            flops=2 * rows * total * hidden * width,
            bytes_accessed=12 * rows * total * width,
            transcendentals=0,
        ),
        name="final_stage",
    )(tri, pair, gate, weight)


def gather_blocks(block):
    devs = lax.axis_size("row")
    if devs != 16:
        return lax.all_gather(block, "row", axis=0)

    def hop(value, step):
        return lax.ppermute(value, "row", [(i, (i + step) % devs) for i in range(devs)])

    def flip(value, bit):
        return lax.ppermute(value, "row", [(i, i ^ bit) for i in range(devs)])

    held = jnp.stack([block, hop(block, 4), hop(block, 8), hop(block, 12)])
    held = jnp.stack([held, flip(held, 2)], axis=1)
    held = jnp.stack([held, flip(held, 1)], axis=2)
    me = lax.axis_index("row")
    z, y, core = me // 4, (me // 2) % 2, me % 2
    place = jnp.arange(devs)
    source = ((z - place // 4) % 4) * 4 + ((y ^ (place // 2 % 2)) * 2) + (core ^ (place % 2))
    slot = jnp.argsort(source)
    return jnp.take(held.reshape((devs,) + block.shape), slot, axis=0)


def body(
    homolog_features,
    coverage_indicator,
    couple_features,
    observed_indicator,
    first_factor_matrix,
    second_factor_matrix,
    product_final_matrix,
    edge_projection_matrix,
    sigmoid_filter_matrix,
    multiplicative_final_matrix,
):
    seqs, rows, breadth = homolog_features.shape
    proj = first_factor_matrix.shape[1]
    width = couple_features.shape[2]
    hidden = multiplicative_final_matrix.shape[0]
    total = observed_indicator.shape[0]
    devs = lax.axis_size("row")
    chans = hidden // devs

    covered = coverage_indicator.astype(F32)
    msa_norm = standardize(homolog_features.astype(F32), -1).astype(BF16)

    def project(weight):
        value = jnp.einsum("sif,fp->sip", msa_norm, weight, preferred_element_type=F32)
        return (value * covered[..., None]).astype(BF16)

    right = project(second_factor_matrix).reshape(seqs, rows, proj // 2, 2)
    right = right.transpose(2, 1, 3, 0).reshape(proj // 2, rows, 2 * seqs)
    mask = jnp.pad(covered.T.astype(BF16), ((0, 0), (0, seqs)))
    gathered = gather_blocks(jnp.concatenate([right, mask[None]]))

    left = project(first_factor_matrix).transpose(1, 2, 0).reshape(rows * proj, seqs)
    left = jnp.concatenate(
        [jnp.pad(left, ((0, 0), (0, seqs))), jnp.pad(left, ((0, 0), (seqs, 0)))]
    )
    w_out = product_final_matrix.reshape(proj, proj, width).transpose(2, 1, 0)
    w_out = w_out.reshape(width, proj * proj)

    seen = observed_indicator.astype(F32)
    start = lax.axis_index("row") * rows
    obs = lax.dynamic_slice_in_dim(seen, start, rows)[:, None] * seen[None, :]

    pair, norm, side_a, side_b = pair_stage(
        left, gathered, mask, couple_features, w_out, edge_projection_matrix.T, obs
    )

    def spread(side):
        side = side.reshape(devs, chans, rows, total)
        return lax.all_to_all(side, "row", split_axis=0, concat_axis=0, tiled=True)

    tri = tri_stage(spread(side_a), spread(side_b))
    gate = gate_stage(norm, sigmoid_filter_matrix.T)
    tri = lax.all_to_all(tri, "row", split_axis=0, concat_axis=0, tiled=True)
    return final_stage(
        tri.reshape(hidden, rows, total), pair, gate, multiplicative_final_matrix.T
    )


def solution(mesh):
    placed = (
        P(None, ("groups", "row"), None),
        P(None, ("groups", "row")),
        P(("groups", "row"), None, None),
        P("groups"),
        P(),
        P(),
        P(),
        P(),
        P(),
        P(),
    )
    return jax.shard_map(
        body,
        mesh=mesh,
        in_specs=placed,
        out_specs=P(("groups", "row"), None, None),
        check_vma=False,
    )
```

```python
import jax
import jax.numpy as jnp
from jax import lax
from jax.experimental import pallas as pl
from jax.experimental.pallas import tpu as pltpu
from jax.sharding import PartitionSpec as P

F32 = jnp.float32
BF16 = jnp.bfloat16
LANES = 128
BLOCK = 2 * LANES
PAD = 8
NT = (((1,), (1,)), ((), ()))
MIB = 1024 * 1024


def sigmoid(value):
    return 0.5 * jnp.tanh(0.5 * value) + 0.5


def standardize(value, axis):
    mean = jnp.mean(value, axis=axis, keepdims=True)
    centred = value - mean
    var = jnp.mean(centred * centred, axis=axis, keepdims=True)
    return centred * lax.rsqrt(var + 1e-05)


def local_call(name, kernel, steps, ins, outs, scratch, limit, flops=0, data=0, special=0):
    whole = steps == 1
    in_specs, out_specs, out_shape = [], [], []
    for value, block, index in ins:
        if block is None:
            in_specs.append(pl.BlockSpec(memory_space=pltpu.SMEM))
        elif whole:
            in_specs.append(pl.BlockSpec(memory_space=pltpu.VMEM))
        else:
            in_specs.append(pl.BlockSpec(block, index))
    for shape, dtype, block, index in outs:
        if whole:
            out_specs.append(pl.BlockSpec(memory_space=pltpu.VMEM))
        else:
            out_specs.append(pl.BlockSpec(block, index))
        keep = whole and name != "final_stage"
        out_shape.append(
            pltpu.VMEM(shape, dtype) if keep else jax.ShapeDtypeStruct(shape, dtype)
        )
    return pl.pallas_call(
        kernel,
        grid=() if whole else (steps,),
        in_specs=in_specs,
        out_specs=out_specs,
        out_shape=out_shape,
        scratch_shapes=scratch,
        compiler_params=pltpu.CompilerParams(
            vmem_limit_bytes=(limit if whole else 56) * MIB
        ),
        cost_estimate=pl.CostEstimate(
            flops=flops // 1000, bytes_accessed=data // 1000, transcendentals=special // 1000
        ),
        name=name,
    )(*[value for value, _, _ in ins])


def fixed(value):
    return value, value.shape, lambda j: (0,) * value.ndim


def last(value, block):
    return value, value.shape[:-1] + (block,), lambda j: (0,) * (value.ndim - 1) + (j,)


def last_out(shape, dtype, block):
    return shape, dtype, shape[:-1] + (block,), lambda j: (0,) * (len(shape) - 1) + (j,)


def identity(size, order=lambda row: row):
    row = lax.broadcasted_iota(jnp.int32, (size, size), 0)
    column = lax.broadcasted_iota(jnp.int32, (size, size), 1)
    return (order(row) == column).astype(BF16)


def msa_kernel(msa_ref, cover_ref, left_w_ref, right_w_ref, right_ref, left_ref, values, rights, lefts):
    seqs, rows, breadth = msa_ref.shape
    proj = left_w_ref.shape[0]
    pairs = proj // 2
    tiles = breadth // LANES
    msa = msa_ref[...].astype(F32).reshape(seqs * rows, breadth)
    for tile in range(tiles):
        values[tile] = msa[:, tile * LANES : (tile + 1) * LANES]
    cover = cover_ref[...].astype(F32)
    swap = identity(proj, lambda row: 2 * (row % pairs) + row // pairs)
    right_w = jnp.dot(swap, right_w_ref[...], preferred_element_type=F32).astype(BF16)
    weights = jnp.concatenate([left_w_ref[...], right_w])
    for i in range(rows):
        row = jnp.concatenate(
            [values[tile, pl.ds(i, seqs, stride=rows), :] for tile in range(tiles)], axis=1
        )
        norm = standardize(row, -1).astype(BF16)
        factor = lax.dot_general(weights, norm, NT, preferred_element_type=F32)
        factor = factor * cover[i : i + 1]
        lefts[i] = factor[:proj]
        rights[i * pairs : (i + 1) * pairs] = jnp.concatenate(
            [factor[proj : proj + pairs], factor[proj + pairs :]], axis=1
        )
    half = rows // 2
    for i in range(half):
        left_ref[i * proj : (i + 1) * proj] = jnp.concatenate(
            [lefts[i], lefts[i + half]], axis=1
        ).astype(BF16)
    for t in range(pairs):
        right_ref[t] = rights[pl.ds(t, rows, stride=pairs), :].astype(BF16)
    right_ref[pairs] = jnp.concatenate([cover, jnp.zeros_like(cover)], axis=1).astype(BF16)


def msa_stage(msa, cover, left_w, right_w):
    seqs, rows, breadth = msa.shape
    proj = left_w.shape[0]
    right = (proj // 2 + 1, rows, 2 * seqs)
    left = (rows * proj // 2, 2 * seqs)
    return local_call(
        "msa_stage",
        msa_kernel,
        1,
        [fixed(msa), fixed(cover), fixed(left_w), fixed(right_w)],
        [(right, BF16, None, None), (left, BF16, None, None)],
        [
            pltpu.VMEM((breadth // LANES, seqs * rows, LANES), F32),
            pltpu.VMEM((rows * proj // 2, 2 * seqs), F32),
            pltpu.VMEM((rows, proj, seqs), F32),
        ],
        12,
        flops=4 * seqs * rows * breadth * proj,
        data=2 * seqs * rows * breadth,
    )


def weights_kernel(out_ref, in_ref, gate_ref, final_ref, out_t, in_t, gate_t, final_t, rows):
    one = identity(LANES)

    def turned(value):
        return lax.dot_general(one, value, NT, preferred_element_type=F32).astype(BF16)

    depth, width = out_ref.shape
    proj = int(depth**0.5)
    rows[...] = out_ref[...].astype(F32)
    ordered = jnp.concatenate([rows[pl.ds(q, proj, stride=proj), :] for q in range(proj)])
    out_t[...] = turned(ordered.astype(BF16))
    for k in range(in_ref.shape[1] // LANES):
        cols = slice(k * LANES, (k + 1) * LANES)
        in_t[cols] = turned(in_ref[:, cols])
    gate_t[...] = turned(gate_ref[...])
    final_t[...] = turned(final_ref[...])


def weights_stage(w_out, w_in, w_gate, w_final):
    depth, width = w_out.shape
    shapes = [w_out.shape[::-1], w_in.shape[::-1], w_gate.shape[::-1], w_final.shape[::-1]]
    return local_call(
        "weights_stage",
        weights_kernel,
        1,
        [fixed(w_out), fixed(w_in), fixed(w_gate), fixed(w_final)],
        [(shape, BF16, None, None) for shape in shapes],
        [pltpu.VMEM((depth, width), F32)],
        8,
        flops=2 * LANES * LANES * LANES * 6,
        data=4 * depth * width,
    )


def order_right(right_refs, right):
    me = lax.axis_index("row")
    for index, ref in enumerate(right_refs):
        core, y = index // 2, index % 2
        for z in range(4):
            right[((me // 4 - z) & 3) * 4 + ((me & 3) ^ (2 * y + core))] = ref[z]


def make_updates(left_ref, mask, right, outer, count):
    slices = right.shape[1]
    rows, depth, block = outer.shape
    proj = depth // (2 * (slices - 1))
    count[...] = lax.dot_general(
        mask, right[:, slices - 1].reshape(block, LANES), NT, preferred_element_type=F32
    )
    left = left_ref[...].astype(F32)
    turned = pltpu.roll(left, LANES // 2, 1)
    low = lax.broadcasted_iota(jnp.int32, left.shape, 1) < LANES // 2
    both_left = jnp.concatenate(
        [
            jnp.where(low, left, 0.0),
            jnp.where(low, turned, 0.0),
            jnp.where(low, 0.0, turned),
            jnp.where(low, 0.0, left),
        ]
    ).astype(BF16)
    half = rows * proj

    @pl.loop(0, slices - 1, unroll=4)
    def _(t):
        both = lax.dot_general(
            both_left,
            right[:, pl.ds(t, 1)].reshape(block, LANES),
            NT,
            preferred_element_type=F32,
        ).astype(BF16)
        for e in range(2):
            outer[:, pl.ds(pl.multiple_of((2 * t + e) * proj, proj), proj), :] = both[
                e * half : (e + 1) * half
            ].reshape(rows, proj, block)


def row_update(i, w_out_ref, outer, count):
    update = jnp.dot(w_out_ref[...], outer[i], preferred_element_type=F32)
    return update / jnp.maximum(count[i : i + 1], 1.0)


def chip_here(split):
    return jnp.int32(0) if split == 1 else (lax.axis_index("row") // 2) & (split - 1)


def observed(device, obs_ref, seen_ref, rows, i):
    return seen_ref[...].astype(F32) * obs_ref[device * rows + i].astype(F32)


def keep_sides(i, norm, w_in_ref, seen, sides_of, hidden):
    sides = jnp.dot(w_in_ref[...], norm, preferred_element_type=F32)
    stride = hidden + PAD
    for side, kept in enumerate(sides_of):
        gates = sides[2 * side * hidden : (2 * side + 1) * hidden]
        values = sides[(2 * side + 1) * hidden : (2 * side + 2) * hidden]
        value = sigmoid(gates) * values * seen
        for tile in range(kept.shape[0]):
            kept[tile, i * stride : i * stride + hidden] = value[
                :, tile * LANES : (tile + 1) * LANES
            ]


def write_sides(kept, outs, rows, hidden):
    per, chans = outs[0].shape[:2]
    chip = chip_here(len(outs))
    for part in range(per * len(outs)):
        target = outs[part // per].at[part % per]
        start = (chip ^ part) * chans

        @pl.loop(0, chans, unroll=8 if chans % 8 == 0 else chans)
        def _(c):
            for tile in range(kept.shape[0]):
                target[c, :, tile * LANES : (tile + 1) * LANES] = kept[
                    tile, pl.ds(start + c, rows, stride=hidden + PAD), :
                ].astype(BF16)


def pair_kernel(pieces, split, *refs):
    left_ref, mask_ref, couple_ref, w_out_ref, w_in_ref, w_gate_ref, obs_ref, seen_ref = refs[:8]
    right_refs, refs = refs[8 : 8 + pieces], refs[8 + pieces :]
    pair_ref, gate_ref = refs[:2]
    a_refs, b_refs, refs = refs[2 : 2 + split], refs[2 + split : 2 + 2 * split], refs[2 + 2 * split :]
    if pieces > 1:
        right, refs = refs[0], refs[1:]
        order_right(right_refs, right)
    else:
        right = right_refs[0]
    outer, kept_a, kept_b, count = refs
    rows = couple_ref.shape[0]
    hidden = w_in_ref.shape[0] // 4
    make_updates(left_ref, mask_ref[...], right, outer, count)
    for i in range(rows):
        pair = couple_ref[i].astype(F32).T + row_update(i, w_out_ref, outer, count)
        norm = standardize(pair, 0).astype(BF16)
        pair_ref[i] = pair
        gate_ref[i] = sigmoid(jnp.dot(w_gate_ref[...], norm, preferred_element_type=F32))
        seen = observed(lax.axis_index("row"), obs_ref, seen_ref, rows, i)
        keep_sides(i, norm, w_in_ref, seen, (kept_a, kept_b), hidden)
    write_sides(kept_b, b_refs, rows, hidden)
    write_sides(kept_a, a_refs, rows, hidden)


def update_kernel(left_ref, w_out_ref, right, *refs):
    mask_refs, (update_ref, outer, count) = refs[:-3], refs[-3:]
    if mask_refs:
        mask = mask_refs[0][...]
    else:
        mask = right[lax.axis_index("row") ^ 12, right.shape[1] - 1]
    make_updates(left_ref, mask, right, outer, count)
    for i in range(update_ref.shape[0]):
        update_ref[i] = row_update(i, w_out_ref, outer, count)


def mirror_kernel(low, mirror, update_ref, couple_ref, w_in_ref, obs_ref, seen_ref, *refs):
    outs, kept = refs[:-1], refs[-1]
    rows, block = update_ref.shape[0], couple_ref.shape[1]
    hidden = w_in_ref.shape[0] // 4
    cols = slice(low, low + block)
    for i in range(rows):
        pair = couple_ref[i].astype(F32).T + update_ref[i, :, cols]
        device = mirror(lax.axis_index("row"))
        seen = observed(device, obs_ref, seen_ref, rows, i)[:, cols]
        norm = standardize(pair, 0).astype(BF16)
        keep_sides(i, norm, w_in_ref.at[2 * hidden :], seen, (kept,), hidden)
    write_sides(kept, outs, rows, hidden)


def right_input(value, total):
    return value, (value.shape[0] * BLOCK // total,) + value.shape[1:], lambda j: (j, 0, 0, 0)


def couple_input(couple):
    return couple, (couple.shape[0], BLOCK, couple.shape[2]), lambda j: (0, j, 0)


def kept_scratch(rows, hidden, block):
    return pltpu.VMEM((block // LANES, rows * (hidden + PAD), LANES), F32)


def scalars(value):
    return value, None, None


def pair_stage(left, right, mask, couple, w_out, w_in, w_gate, obs, parts, split):
    rows, total, width = couple.shape
    hidden = w_in.shape[0] // 4
    piece = (parts // split, hidden // parts, rows, total)
    outs = [last_out((rows, width, total), F32, BLOCK)] * 2
    outs += [last_out(piece, BF16, BLOCK)] * (2 * split)
    if len(right) > 1:
        outs += [((total // rows,) + right[0].shape[1:], BF16, None, None)]
    return local_call(
        "pair_stage",
        lambda *refs: pair_kernel(len(right), split, *refs),
        total // BLOCK,
        [fixed(left), fixed(mask), couple_input(couple), fixed(w_out), fixed(w_in)]
        + [fixed(w_gate), scalars(obs), last(obs[None], BLOCK)]
        + [right_input(value, total) for value in right],
        outs,
        [pltpu.VMEM((rows, w_out.shape[1], BLOCK), BF16)]
        + [kept_scratch(rows, hidden, BLOCK)] * 2
        + [pltpu.VMEM((rows, BLOCK), F32)],
        24,
        flops=4 * rows * total * w_out.shape[1] * width,
        data=16 * rows * total * width,
        special=3 * rows * total * hidden,
    )


def update_stage(left, right, mask, w_out, rows, total):
    width = w_out.shape[0]
    return local_call(
        "update_stage",
        update_kernel,
        total // BLOCK,
        [fixed(left), fixed(w_out), right_input(right, total)]
        + ([] if mask is None else [fixed(mask)]),
        [last_out((rows, width, total), F32, BLOCK)],
        [pltpu.VMEM((rows, w_out.shape[1], BLOCK), BF16), pltpu.VMEM((rows, BLOCK), F32)],
        20,
        flops=4 * rows * total * w_out.shape[1] * width,
        data=8 * rows * total * width,
    )[0]


def mirror_stage(low, mirror, update, couple, w_in, obs, parts, split):
    rows, width = update.shape[:2]
    total = couple.shape[1]
    hidden = w_in.shape[0] // 4
    block = min(BLOCK, total)
    return local_call(
        "mirror_stage",
        lambda *refs: mirror_kernel(low, mirror, *refs),
        total // block,
        [last(update, block), couple_input(couple), fixed(w_in), scalars(obs)]
        + [last(obs[None], block)],
        [last_out((parts // split, hidden // parts, rows, total), BF16, block)] * split,
        [kept_scratch(rows, hidden, block)],
        16,
        flops=4 * rows * total * hidden * width,
        data=8 * rows * total * width,
        special=rows * total * hidden,
    )


def tri_kernel(cores, split, cuts, flip, *refs):
    a_refs, refs = refs[:split], refs[split:]
    b_refs = [refs[cut * cores * split : (cut + 1) * cores * split] for cut in range(cuts)]
    outs, whole = refs[cuts * cores * split : -1], refs[-1]
    per, chans, rows, total = a_refs[0].shape
    depth = total // cuts
    chip = chip_here(split)
    core = lax.axis_index("row") & 1
    for c in range(chans):
        for cut in range(cuts):
            for index, ref in enumerate(b_refs[cut]):
                for slot in range(per):
                    part = (index % split) * per + slot
                    place = (chip ^ part ^ flip) * cores
                    if cores == 2:
                        place = place + (core ^ (index // split))
                    place = pl.multiple_of(place * rows, rows)
                    whole[c, pl.ds(place, rows), cut * depth : (cut + 1) * depth] = ref[slot, c]
        side_a = jnp.concatenate([ref[slot, c] for ref in a_refs for slot in range(per)])
        product = lax.dot_general(side_a, whole[c], NT, preferred_element_type=F32).astype(BF16)
        for part in range(per * split):
            outs[part // per][part % per, c] = product[part * rows : (part + 1) * rows]


def channels(value, step):
    return value, value.shape[:1] + (step,) + value.shape[2:], lambda c: (0, c, 0, 0)


def tri_stage(a, b, cores, flip):
    split = len(a)
    per, chans, rows, total = a[0].shape
    step = max(1, min(chans, chans * BLOCK // total))
    half = per * split * cores * rows
    shape = (per, chans, rows, half)
    return local_call(
        "tri_stage",
        lambda *refs: tri_kernel(cores, split, len(b), flip, *refs),
        chans // step,
        [channels(value, step) for value in a]
        + [channels(value, step) for cut in b for value in cut],
        [(shape, BF16, (per, step, rows, half), lambda c: (0, c, 0, 0))] * split,
        [pltpu.VMEM((step, half, total), BF16)],
        16,
        flops=2 * chans * per * split * rows * half * total,
        data=6 * chans * half * total,
    )


def final_kernel(spans, split, pair_ref, gate_ref, w_ref, *refs):
    out_ref, normed = refs[-2:]
    rows, _, whole = pair_ref.shape
    per, chans, _, block = refs[0].shape
    parts = per * split
    hidden = chans * parts
    tiles = block // LANES
    chip = chip_here(split)
    for span in range(spans):
        tri = refs[span * split : (span + 1) * split]
        if spans == 1:
            low = 0
        else:
            devs = lax.axis_size("row")
            mine = lax.div(lax.axis_index("row"), devs // 2)
            low = pl.multiple_of((mine ^ span) * block, block)
        values = standardize(
            jnp.concatenate([ref[slot] for ref in tri for slot in range(per)]).astype(F32), 0
        )
        for part in range(parts):
            first = pl.multiple_of((chip ^ part) * (chans * rows), chans * rows)
            for tile in range(tiles):
                normed[tile, pl.ds(first, chans * rows), :] = values[
                    part * chans : (part + 1) * chans, :, tile * LANES : (tile + 1) * LANES
                ].reshape(chans * rows, LANES)
        for i in range(rows):
            columns = jnp.concatenate(
                [normed[tile, pl.ds(i, hidden, stride=rows), :] for tile in range(tiles)], axis=1
            ).astype(BF16)
            update = jnp.dot(w_ref[...], columns, preferred_element_type=F32)
            cols = pl.ds(low, block)
            result = pair_ref[i, :, cols] + gate_ref[i, :, cols] * update
            out_ref[i, cols, :] = result.T.astype(BF16)


def final_stage(spans, pair, gate, weight):
    rows, width, total = pair.shape
    hidden = weight.shape[1]
    split = len(spans[0])
    block = spans[0][0].shape[-1] if len(spans) > 1 else BLOCK
    return local_call(
        "final_stage",
        lambda *refs: final_kernel(len(spans), split, *refs),
        total // BLOCK,
        [last(pair, BLOCK), last(gate, BLOCK), fixed(weight)]
        + [last(value, block) for span in spans for value in span],
        [((rows, total, width), BF16, (rows, BLOCK, width), lambda j: (0, j, 0))],
        [pltpu.VMEM((block // LANES, hidden * rows, LANES), F32)],
        24,
        flops=2 * rows * total * hidden * width,
        data=12 * rows * total * width,
    )[0]


def send(value, move):
    devs = lax.axis_size("row")
    return lax.ppermute(value, "row", [(i, move(i)) for i in range(devs)])


def after(first, value):
    return lax.optimization_barrier((first, value))


def exchange(pieces, earlier=None):
    devs = lax.axis_size("row")
    half = devs // 2
    if len(pieces) == 1:
        groups = [list(range(half)), list(range(half, devs))]
        return [
            lax.all_to_all(
                pieces[0], "row", split_axis=0, concat_axis=0, tiled=True, axis_index_groups=groups
            )
        ]
    out = list(pieces)
    for r in range(1, len(out)):
        if earlier is not None:
            _, out[r] = after(earlier[r], out[r])
        out[r] = send(out[r], lambda i, r=r: i ^ (2 * r))
    return out


def with_other_core(pieces):
    if len(pieces) == 1:
        return pieces
    return list(pieces) + [send(value, lambda i: i ^ 1) for value in pieces]


def body(
    homolog_features,
    coverage_indicator,
    couple_features,
    observed_indicator,
    first_factor_matrix,
    second_factor_matrix,
    product_final_matrix,
    edge_projection_matrix,
    sigmoid_filter_matrix,
    multiplicative_final_matrix,
):
    rows, total, width = couple_features.shape
    devs = lax.axis_size("row")
    half = devs // 2
    me = lax.axis_index("row")
    hops = devs == 16
    cores, cuts = (2, 2) if hops else (1, 1)
    parts = half // cores
    split = parts if hops else 1
    obs = observed_indicator

    def mirror(device):
        return device ^ 12 if hops else (device + half) % devs

    def mirrored(value):
        return send(value, mirror)

    block, left = msa_stage(
        homolog_features,
        coverage_indicator.T,
        first_factor_matrix.T,
        second_factor_matrix.T,
    )
    couples = [
        couple_features[:, cut * total // cuts : (cut + 1) * total // cuts] for cut in range(cuts)
    ]
    if hops:
        couples[0] = jnp.concatenate([couples[0], left.reshape(-1, total // cuts, width)])
    weights = weights_stage(
        product_final_matrix,
        edge_projection_matrix,
        sigmoid_filter_matrix,
        multiplicative_final_matrix,
    )
    if hops:
        held = [block] + [send(block, lambda i, d=d: (i + 4 * d) % devs) for d in (1, 2, 3)]
        held, (*couples, weights) = after(jnp.stack(held), (*couples, weights))
        other = send(held, lambda i: i ^ 2)
        right = [held, other, send(held, lambda i: i ^ 1), send(other, lambda i: i ^ 1)]
        far_mask = None
    else:
        right = [lax.all_gather(block, "row", axis=0)]
        far_left = mirrored(left)
        far_mask = right[0][mirror(me), -1]
    far_couples = [mirrored(value) for value in couples]
    if hops:
        far_left = far_couples[0][rows:].reshape(left.shape)
    w_out, w_in, w_gate, w_final = weights

    pair, gate, *sides = pair_stage(
        left, right, block[-1], couple_features, w_out, w_in, w_gate, obs, parts, split
    )
    a, b = sides[:split], sides[split : 2 * split]
    ordered = sides[2 * split] if hops else right[0]
    b = exchange(b)
    update = update_stage(far_left, ordered, far_mask, w_out, rows, total)
    if hops:
        update, b = after(update, b)
    a = exchange(a, b)
    b = with_other_core(b)
    near = exchange(tri_stage(a, [b], cores, 0))
    far_b = []
    for cut, value in enumerate(far_couples):
        low = cut * total // cuts
        sides = mirror_stage(low, mirror, update, value, w_in, obs, parts, split)
        far_b.append(with_other_core(exchange(sides, a)))
    far = exchange(tri_stage(a, far_b, cores, 2 if hops else 0))
    if hops:
        spans = [near, far]
    else:
        lower = me < half
        spans = [
            [
                jnp.concatenate(
                    [jnp.where(lower, x, y), jnp.where(lower, y, x)], axis=-1
                )
                for x, y in zip(near, far)
            ]
        ]
    return final_stage(spans, pair, gate, w_final)


def solution(mesh):
    placed = (
        P(None, ("groups", "row"), None),
        P(None, ("groups", "row")),
        P(("groups", "row"), None, None),
        P("groups"),
        P(),
        P(),
        P(),
        P(),
        P(),
        P(),
    )
    return jax.shard_map(
        body,
        mesh=mesh,
        in_specs=placed,
        out_specs=P(("groups", "row"), None, None),
        check_vma=False,
    )
```

```python
import jax
import jax.numpy as jnp
from jax import lax
from jax.experimental import pallas as pl
from jax.experimental.pallas import tpu as pltpu
from jax.sharding import PartitionSpec as P

F32 = jnp.float32
BF16 = jnp.bfloat16
LANES = 128
BLOCK = 2 * LANES
PAD = 8
NT = (((1,), (1,)), ((), ()))
MIB = 1024 * 1024


def sigmoid(value):
    return 0.5 * jnp.tanh(0.5 * value) + 0.5


def standardize(value, axis):
    mean = jnp.mean(value, axis=axis, keepdims=True)
    centred = value - mean
    var = jnp.mean(centred * centred, axis=axis, keepdims=True)
    return centred * lax.rsqrt(var + 1e-05)


def local_call(name, kernel, steps, ins, outs, scratch, limit, flops=0, data=0, special=0, windows=False):
    whole = steps == 1
    in_specs, out_specs, out_shape = [], [], []
    for value, block, index in ins:
        if block is None:
            in_specs.append(pl.BlockSpec(memory_space=pltpu.SMEM))
        elif whole and windows:
            in_specs.append(pl.BlockSpec(value.shape, lambda ndim=value.ndim: (0,) * ndim))
        elif whole:
            in_specs.append(pl.BlockSpec(memory_space=pltpu.VMEM))
        else:
            in_specs.append(pl.BlockSpec(block, index))
    for shape, dtype, block, index in outs:
        if whole:
            out_specs.append(pl.BlockSpec(memory_space=pltpu.VMEM))
        else:
            out_specs.append(pl.BlockSpec(block, index))
        keep = whole and name != "final_stage"
        out_shape.append(
            pltpu.VMEM(shape, dtype) if keep else jax.ShapeDtypeStruct(shape, dtype)
        )
    return pl.pallas_call(
        kernel,
        grid=() if whole else (steps,),
        in_specs=in_specs,
        out_specs=out_specs,
        out_shape=out_shape,
        scratch_shapes=scratch,
        compiler_params=pltpu.CompilerParams(
            vmem_limit_bytes=(limit if whole else 56) * MIB
        ),
        cost_estimate=pl.CostEstimate(
            flops=flops // 1000, bytes_accessed=data // 1000, transcendentals=special // 1000
        ),
        name=name,
    )(*[value for value, _, _ in ins])


def fixed(value):
    return value, value.shape, lambda j: (0,) * value.ndim


def last(value, block):
    return value, value.shape[:-1] + (block,), lambda j: (0,) * (value.ndim - 1) + (j,)


def last_out(shape, dtype, block):
    return shape, dtype, shape[:-1] + (block,), lambda j: (0,) * (len(shape) - 1) + (j,)


def identity(size, order=lambda row: row):
    row = lax.broadcasted_iota(jnp.int32, (size, size), 0)
    column = lax.broadcasted_iota(jnp.int32, (size, size), 1)
    return (order(row) == column).astype(BF16)


def msa_kernel(msa_ref, cover_ref, left_w_ref, right_w_ref, right_ref, left_ref, values, rights, lefts):
    seqs, rows, breadth = msa_ref.shape
    proj = left_w_ref.shape[0]
    pairs = proj // 2
    tiles = breadth // LANES
    msa = msa_ref[...].astype(F32).reshape(seqs * rows, breadth)
    for tile in range(tiles):
        values[tile] = msa[:, tile * LANES : (tile + 1) * LANES]
    cover = cover_ref[...].astype(F32)
    swap = identity(proj, lambda row: 2 * (row % pairs) + row // pairs)
    right_w = jnp.dot(swap, right_w_ref[...], preferred_element_type=F32).astype(BF16)
    weights = jnp.concatenate([left_w_ref[...], right_w])
    for i in range(rows):
        row = jnp.concatenate(
            [values[tile, pl.ds(i, seqs, stride=rows), :] for tile in range(tiles)], axis=1
        )
        norm = standardize(row, -1).astype(BF16)
        factor = lax.dot_general(weights, norm, NT, preferred_element_type=F32)
        factor = factor * cover[i : i + 1]
        lefts[i] = factor[:proj]
        rights[i * pairs : (i + 1) * pairs] = jnp.concatenate(
            [factor[proj : proj + pairs], factor[proj + pairs :]], axis=1
        )
    half = rows // 2
    for i in range(half):
        left_ref[i * proj : (i + 1) * proj] = jnp.concatenate(
            [lefts[i], lefts[i + half]], axis=1
        ).astype(BF16)
    for t in range(pairs):
        right_ref[t] = rights[pl.ds(t, rows, stride=pairs), :].astype(BF16)
    right_ref[pairs] = jnp.concatenate([cover, jnp.zeros_like(cover)], axis=1).astype(BF16)


def msa_stage(msa, cover, left_w, right_w):
    seqs, rows, breadth = msa.shape
    proj = left_w.shape[0]
    right = (proj // 2 + 1, rows, 2 * seqs)
    left = (rows * proj // 2, 2 * seqs)
    return local_call(
        "msa_stage",
        msa_kernel,
        1,
        [fixed(msa), fixed(cover), fixed(left_w), fixed(right_w)],
        [(right, BF16, None, None), (left, BF16, None, None)],
        [
            pltpu.VMEM((breadth // LANES, seqs * rows, LANES), F32),
            pltpu.VMEM((rows * proj // 2, 2 * seqs), F32),
            pltpu.VMEM((rows, proj, seqs), F32),
        ],
        12,
        flops=4 * seqs * rows * breadth * proj,
        data=2 * seqs * rows * breadth,
        windows=True,
    )


def weights_kernel(out_ref, in_ref, gate_ref, final_ref, out_t, in_t, gate_t, final_t, rows):
    one = identity(LANES)

    def turned(value):
        return lax.dot_general(one, value, NT, preferred_element_type=F32).astype(BF16)

    depth, width = out_ref.shape
    proj = int(depth**0.5)
    rows[...] = out_ref[...].astype(F32)
    ordered = jnp.concatenate([rows[pl.ds(q, proj, stride=proj), :] for q in range(proj)])
    out_t[...] = turned(ordered.astype(BF16))
    for k in range(in_ref.shape[1] // LANES):
        cols = slice(k * LANES, (k + 1) * LANES)
        in_t[cols] = turned(in_ref[:, cols])
    gate_t[...] = turned(gate_ref[...])
    final_t[...] = turned(final_ref[...])


def weights_stage(w_out, w_in, w_gate, w_final):
    depth, width = w_out.shape
    shapes = [w_out.shape[::-1], w_in.shape[::-1], w_gate.shape[::-1], w_final.shape[::-1]]
    return local_call(
        "weights_stage",
        weights_kernel,
        1,
        [fixed(w_out), fixed(w_in), fixed(w_gate), fixed(w_final)],
        [(shape, BF16, None, None) for shape in shapes],
        [pltpu.VMEM((depth, width), F32)],
        8,
        flops=2 * LANES * LANES * LANES * 6,
        data=4 * depth * width,
    )


def order_right(right_refs, right):
    me = lax.axis_index("row")
    for index, ref in enumerate(right_refs):
        core, y = index // 2, index % 2
        for z in range(4):
            right[me ^ (4 * z + 2 * y + core)] = ref[z]


def make_updates(left_ref, mask, right, outer, scale):
    slices = right.shape[1]
    rows, depth, block = outer.shape
    proj = depth // (2 * (slices - 1))
    count = lax.dot_general(
        mask, right[:, slices - 1].reshape(block, LANES), NT, preferred_element_type=F32
    )
    scale[...] = 1.0 / jnp.maximum(count, 1.0)
    left = left_ref[...].astype(F32)
    turned = pltpu.roll(left, LANES // 2, 1)
    low = lax.broadcasted_iota(jnp.int32, left.shape, 1) < LANES // 2
    both_left = jnp.concatenate(
        [
            jnp.where(low, left, 0.0),
            jnp.where(low, turned, 0.0),
            jnp.where(low, 0.0, turned),
            jnp.where(low, 0.0, left),
        ]
    ).astype(BF16)
    half = rows * proj

    @pl.loop(0, slices - 1, unroll=4)
    def _(t):
        both = lax.dot_general(
            both_left,
            right[:, pl.ds(t, 1)].reshape(block, LANES),
            NT,
            preferred_element_type=F32,
        ).astype(BF16)
        for e in range(2):
            outer[:, pl.ds(pl.multiple_of((2 * t + e) * proj, proj), proj), :] = both[
                e * half : (e + 1) * half
            ].reshape(rows, proj, block)


def row_update(i, w_out_ref, outer, scale):
    update = jnp.dot(w_out_ref[...], outer[i], preferred_element_type=F32)
    return update * scale[i : i + 1]


def chip_here(split):
    return jnp.int32(0) if split == 1 else (lax.axis_index("row") // 2) & (split - 1)


def observed(device, obs_ref, seen_ref, rows, i):
    return seen_ref[...].astype(F32) * obs_ref[device * rows + i].astype(F32)


def keep_sides(i, norm, w_in_ref, seen, sides_of, hidden):
    sides = jnp.dot(w_in_ref[...], norm, preferred_element_type=F32)
    stride = hidden + PAD
    for side, kept in enumerate(sides_of):
        gates = sides[2 * side * hidden : (2 * side + 1) * hidden]
        values = sides[(2 * side + 1) * hidden : (2 * side + 2) * hidden]
        value = sigmoid(gates) * values * seen
        for tile in range(kept.shape[0]):
            kept[tile, i * stride : i * stride + hidden] = value[
                :, tile * LANES : (tile + 1) * LANES
            ]


def write_sides(kept, outs, rows, hidden):
    per, chans = outs[0].shape[:2]
    chip = chip_here(len(outs))
    for part in range(per * len(outs)):
        target = outs[part // per].at[part % per]
        start = (chip ^ part) * chans

        @pl.loop(0, chans, unroll=8 if chans % 8 == 0 else chans)
        def _(c):
            for tile in range(kept.shape[0]):
                target[c, :, tile * LANES : (tile + 1) * LANES] = kept[
                    tile, pl.ds(start + c, rows, stride=hidden + PAD), :
                ].astype(BF16)


def pair_kernel(pieces, split, *refs):
    left_ref, mask_ref, couple_ref, w_out_ref, w_in_ref, w_gate_ref, obs_ref, seen_ref = refs[:8]
    right_refs, refs = refs[8 : 8 + pieces], refs[8 + pieces :]
    pair_ref, gate_ref = refs[:2]
    a_refs, b_refs, refs = refs[2 : 2 + split], refs[2 + split : 2 + 2 * split], refs[2 + 2 * split :]
    if pieces > 1:
        right, refs = refs[0], refs[1:]
        order_right(right_refs, right)
    else:
        right = right_refs[0]
    outer, kept_a, kept_b, scale = refs
    rows = couple_ref.shape[0]
    hidden = w_in_ref.shape[0] // 4
    make_updates(left_ref, mask_ref[...], right, outer, scale)
    for i in range(rows):
        pair = couple_ref[i].astype(F32).T + row_update(i, w_out_ref, outer, scale)
        norm = standardize(pair, 0).astype(BF16)
        pair_ref[i] = pair
        gate_ref[i] = sigmoid(jnp.dot(w_gate_ref[...], norm, preferred_element_type=F32))
        seen = observed(lax.axis_index("row"), obs_ref, seen_ref, rows, i)
        keep_sides(i, norm, w_in_ref, seen, (kept_a, kept_b), hidden)
    write_sides(kept_b, b_refs, rows, hidden)
    write_sides(kept_a, a_refs, rows, hidden)


def update_kernel(left_ref, w_out_ref, right, *refs):
    mask_refs, (update_ref, outer, scale) = refs[:-3], refs[-3:]
    if mask_refs:
        mask = mask_refs[0][...]
    else:
        mask = right[lax.axis_index("row") ^ 12, right.shape[1] - 1]
    make_updates(left_ref, mask, right, outer, scale)
    for i in range(update_ref.shape[0]):
        update_ref[i] = row_update(i, w_out_ref, outer, scale)


def mirror_kernel(mirror, update_ref, couple_ref, w_in_ref, obs_ref, seen_ref, *refs):
    outs, kept = refs[:-1], refs[-1]
    rows = couple_ref.shape[0]
    hidden = w_in_ref.shape[0] // 4
    for i in range(rows):
        pair = couple_ref[i].astype(F32).T + update_ref[i]
        device = mirror(lax.axis_index("row"))
        seen = observed(device, obs_ref, seen_ref, rows, i)
        norm = standardize(pair, 0).astype(BF16)
        keep_sides(i, norm, w_in_ref.at[2 * hidden :], seen, (kept,), hidden)
    write_sides(kept, outs, rows, hidden)


def right_input(value, total):
    return value, (value.shape[0] * BLOCK // total,) + value.shape[1:], lambda j: (j, 0, 0, 0)


def couple_input(couple):
    return couple, (couple.shape[0], BLOCK, couple.shape[2]), lambda j: (0, j, 0)


def kept_scratch(rows, hidden, block):
    return pltpu.VMEM((block // LANES, rows * (hidden + PAD), LANES), F32)


def scalars(value):
    return value, None, None


def pair_stage(left, right, mask, couple, w_out, w_in, w_gate, obs, parts, split):
    rows, total, width = couple.shape
    hidden = w_in.shape[0] // 4
    piece = (parts // split, hidden // parts, rows, total)
    outs = [last_out((rows, width, total), F32, BLOCK)] * 2
    outs += [last_out(piece, BF16, BLOCK)] * (2 * split)
    if len(right) > 1:
        outs += [((total // rows,) + right[0].shape[1:], BF16, None, None)]
    return local_call(
        "pair_stage",
        lambda *refs: pair_kernel(len(right), split, *refs),
        total // BLOCK,
        [fixed(left), fixed(mask), couple_input(couple), fixed(w_out), fixed(w_in)]
        + [fixed(w_gate), scalars(obs), last(obs[None], BLOCK)]
        + [right_input(value, total) for value in right],
        outs,
        [pltpu.VMEM((rows, w_out.shape[1], BLOCK), BF16)]
        + [kept_scratch(rows, hidden, BLOCK)] * 2
        + [pltpu.VMEM((rows, BLOCK), F32)],
        24,
        flops=4 * rows * total * w_out.shape[1] * width,
        data=16 * rows * total * width,
        special=3 * rows * total * hidden,
    )


def update_stage(left, right, mask, w_out, rows, total):
    width = w_out.shape[0]
    return local_call(
        "update_stage",
        update_kernel,
        total // BLOCK,
        [fixed(left), fixed(w_out), right_input(right, total)]
        + ([] if mask is None else [fixed(mask)]),
        [last_out((rows, width, total), F32, BLOCK)],
        [pltpu.VMEM((rows, w_out.shape[1], BLOCK), BF16), pltpu.VMEM((rows, BLOCK), F32)],
        20,
        flops=4 * rows * total * w_out.shape[1] * width,
        data=8 * rows * total * width,
    )[0]


def mirror_stage(mirror, update, couple, w_in, obs, parts, split):
    rows, total, width = couple.shape
    hidden = w_in.shape[0] // 4
    return local_call(
        "mirror_stage",
        lambda *refs: mirror_kernel(mirror, *refs),
        total // BLOCK,
        [last(update, BLOCK), couple_input(couple), fixed(w_in), scalars(obs)]
        + [last(obs[None], BLOCK)],
        [last_out((parts // split, hidden // parts, rows, total), BF16, BLOCK)] * split,
        [kept_scratch(rows, hidden, BLOCK)],
        16,
        flops=4 * rows * total * hidden * width,
        data=40000 * rows * total * width,
        special=rows * total * hidden,
    )


def tri_kernel(cores, split, flip, *refs):
    a_refs, refs = refs[:split], refs[split:]
    b_refs, refs = refs[: cores * split], refs[cores * split :]
    outs, whole = refs[:-1], refs[-1]
    per, chans, rows, total = a_refs[0].shape
    chip = chip_here(split)
    core = lax.axis_index("row") & 1
    for c in range(chans):
        for index, ref in enumerate(b_refs):
            for slot in range(per):
                part = (index % split) * per + slot
                place = (chip ^ part ^ flip) * cores
                if cores == 2:
                    place = place + (core ^ (index // split))
                whole[c, pl.ds(pl.multiple_of(place * rows, rows), rows), :] = ref[slot, c]
        side_a = jnp.concatenate([ref[slot, c] for ref in a_refs for slot in range(per)])
        product = lax.dot_general(side_a, whole[c], NT, preferred_element_type=F32).astype(BF16)
        for part in range(per * split):
            outs[part // per][part % per, c] = product[part * rows : (part + 1) * rows]


def channels(value, step):
    return value, value.shape[:1] + (step,) + value.shape[2:], lambda c: (0, c, 0, 0)


def tri_stage(a, b, cores, flip):
    split = len(a)
    per, chans, rows, total = a[0].shape
    step = max(1, min(chans, chans * BLOCK // total))
    half = per * split * cores * rows
    shape = (per, chans, rows, half)
    return local_call(
        "tri_stage",
        lambda *refs: tri_kernel(cores, split, flip, *refs),
        chans // step,
        [channels(value, step) for value in a]
        + [channels(value, step) for value in b],
        [(shape, BF16, (per, step, rows, half), lambda c: (0, c, 0, 0))] * split,
        [pltpu.VMEM((step, half, total), BF16)],
        16,
        flops=2 * chans * per * split * rows * half * total,
        data=6 * chans * half * total,
    )


def final_kernel(spans, split, pair_ref, gate_ref, w_ref, *refs):
    out_ref, normed = refs[-2:]
    rows, _, whole = pair_ref.shape
    per, chans, _, block = refs[0].shape
    parts = per * split
    hidden = chans * parts
    tiles = block // LANES
    chip = chip_here(split)
    for span in range(spans):
        tri = refs[span * split : (span + 1) * split]
        if spans == 1:
            low = 0
        else:
            devs = lax.axis_size("row")
            mine = lax.div(lax.axis_index("row"), devs // 2)
            low = pl.multiple_of((mine ^ span) * block, block)
        values = standardize(
            jnp.concatenate([ref[slot] for ref in tri for slot in range(per)]).astype(F32), 0
        )
        for part in range(parts):
            first = pl.multiple_of((chip ^ part) * (chans * rows), chans * rows)
            for tile in range(tiles):
                normed[tile, pl.ds(first, chans * rows), :] = values[
                    part * chans : (part + 1) * chans, :, tile * LANES : (tile + 1) * LANES
                ].reshape(chans * rows, LANES)
        for i in range(rows):
            columns = jnp.concatenate(
                [normed[tile, pl.ds(i, hidden, stride=rows), :] for tile in range(tiles)], axis=1
            ).astype(BF16)
            update = jnp.dot(w_ref[...], columns, preferred_element_type=F32)
            cols = pl.ds(low, block)
            result = pair_ref[i, :, cols] + gate_ref[i, :, cols] * update
            out_ref[i, cols, :] = result.T.astype(BF16)


def final_stage(spans, pair, gate, weight):
    rows, width, total = pair.shape
    hidden = weight.shape[1]
    split = len(spans[0])
    block = spans[0][0].shape[-1] if len(spans) > 1 else BLOCK
    return local_call(
        "final_stage",
        lambda *refs: final_kernel(len(spans), split, *refs),
        total // BLOCK,
        [last(pair, BLOCK), last(gate, BLOCK), fixed(weight)]
        + [last(value, block) for span in spans for value in span],
        [((rows, total, width), BF16, (rows, BLOCK, width), lambda j: (0, j, 0))],
        [pltpu.VMEM((block // LANES, hidden * rows, LANES), F32)],
        24,
        flops=2 * rows * total * hidden * width,
        data=12 * rows * total * width,
    )[0]


def send(value, move):
    devs = lax.axis_size("row")
    return lax.ppermute(value, "row", [(i, move(i)) for i in range(devs)])


def after(first, value):
    return lax.optimization_barrier((first, value))


def exchange(pieces, earlier=None):
    devs = lax.axis_size("row")
    half = devs // 2
    if len(pieces) == 1:
        groups = [list(range(half)), list(range(half, devs))]
        return [
            lax.all_to_all(
                pieces[0], "row", split_axis=0, concat_axis=0, tiled=True, axis_index_groups=groups
            )
        ]
    out = list(pieces)
    for r in range(1, len(out)):
        if earlier is not None:
            _, out[r] = after(earlier[r], out[r])
        out[r] = send(out[r], lambda i, r=r: i ^ (2 * r))
    return out


def with_other_core(pieces):
    if len(pieces) == 1:
        return pieces
    return list(pieces) + [send(value, lambda i: i ^ 1) for value in pieces]


def body(
    homolog_features,
    coverage_indicator,
    couple_features,
    observed_indicator,
    first_factor_matrix,
    second_factor_matrix,
    product_final_matrix,
    edge_projection_matrix,
    sigmoid_filter_matrix,
    multiplicative_final_matrix,
):
    rows, total, width = couple_features.shape
    devs = lax.axis_size("row")
    half = devs // 2
    me = lax.axis_index("row")
    hops = devs == 16
    cores = 2 if hops else 1
    parts = half // cores
    split = parts if hops else 1
    obs = observed_indicator

    def mirror(device):
        return device ^ 12 if hops else (device + half) % devs

    def mirrored(value):
        return send(value, mirror)

    block, left = msa_stage(
        homolog_features,
        coverage_indicator.T,
        first_factor_matrix.T,
        second_factor_matrix.T,
    )
    weights = weights_stage(
        product_final_matrix,
        edge_projection_matrix,
        sigmoid_filter_matrix,
        multiplicative_final_matrix,
    )
    if hops:
        slices = block.shape[0]
        both = send(jnp.concatenate([block, left.reshape((-1,) + block.shape[1:])]), mirror)
        held = [block, send(block, lambda i: i ^ 4), send(block, lambda i: i ^ 8), both[:slices]]
        far_left = both[slices:].reshape(left.shape)
        held, (couple_out, weights) = after(jnp.stack(held), (couple_features, weights))
        far_couple = mirrored(couple_out)
        other = send(held, lambda i: i ^ 2)
        right = [held, other, send(held, lambda i: i ^ 1), send(other, lambda i: i ^ 1)]
        far_mask = None
    else:
        right = [lax.all_gather(block, "row", axis=0)]
        far_left = mirrored(left)
        far_couple = mirrored(couple_features)
        far_mask = right[0][mirror(me), -1]
    w_out, w_in, w_gate, w_final = weights

    pair, gate, *sides = pair_stage(
        left, right, block[-1], couple_features, w_out, w_in, w_gate, obs, parts, split
    )
    a, b = list(sides[:split]), list(sides[split : 2 * split])
    ordered = sides[2 * split] if hops else right[0]
    b = exchange(b)
    a = exchange(a, b)
    if hops:
        _, far_left = after(b[1], far_left)
    update = update_stage(far_left, ordered, far_mask, w_out, rows, total)
    if hops:
        update, b = after(update, b)
    near = tri_stage(a, with_other_core(b), cores, 0)
    far_b = mirror_stage(mirror, update, far_couple, w_in, obs, parts, split)
    far_b = with_other_core(exchange(far_b, a))
    near = exchange(near)
    far = exchange(tri_stage(a, far_b, cores, 2 if hops else 0))
    if hops:
        spans = [near, far]
    else:
        lower = me < half
        spans = [
            [
                jnp.concatenate(
                    [jnp.where(lower, x, y), jnp.where(lower, y, x)], axis=-1
                )
                for x, y in zip(near, far)
            ]
        ]
    return final_stage(spans, pair, gate, w_final)


def solution(mesh):
    placed = (
        P(None, ("groups", "row"), None),
        P(None, ("groups", "row")),
        P(("groups", "row"), None, None),
        P("groups"),
        P(),
        P(),
        P(),
        P(),
        P(),
        P(),
    )
    return jax.shard_map(
        body,
        mesh=mesh,
        in_specs=placed,
        out_specs=P(("groups", "row"), None, None),
        check_vma=False,
    )
```

```python
import jax
import jax.numpy as jnp
from jax import lax
from jax.experimental import pallas as pl
from jax.experimental.pallas import tpu as pltpu
from jax.sharding import PartitionSpec as P

F32 = jnp.float32
BF16 = jnp.bfloat16
LANES = 128
BLOCK = 2 * LANES
PAD = 8
NT = (((1,), (1,)), ((), ()))
MIB = 1024 * 1024


def sigmoid(value):
    return 0.5 * jnp.tanh(0.5 * value) + 0.5


def standardize(value, axis):
    mean = jnp.mean(value, axis=axis, keepdims=True)
    centred = value - mean
    var = jnp.mean(centred * centred, axis=axis, keepdims=True)
    return centred * lax.rsqrt(var + 1e-05)


def local_call(name, kernel, steps, ins, outs, scratch, limit, flops=0, data=0, special=0, windows=False):
    whole = steps == 1
    in_specs, out_specs, out_shape = [], [], []
    for value, block, index in ins:
        if block is None:
            in_specs.append(pl.BlockSpec(memory_space=pltpu.SMEM))
        elif whole and windows:
            in_specs.append(pl.BlockSpec(value.shape, lambda ndim=value.ndim: (0,) * ndim))
        elif whole:
            in_specs.append(pl.BlockSpec(memory_space=pltpu.VMEM))
        else:
            in_specs.append(pl.BlockSpec(block, index))
    for shape, dtype, block, index in outs:
        if whole:
            out_specs.append(pl.BlockSpec(memory_space=pltpu.VMEM))
        else:
            out_specs.append(pl.BlockSpec(block, index))
        keep = whole and name != "final_stage"
        out_shape.append(
            pltpu.VMEM(shape, dtype) if keep else jax.ShapeDtypeStruct(shape, dtype)
        )
    return pl.pallas_call(
        kernel,
        grid=() if whole else (steps,),
        in_specs=in_specs,
        out_specs=out_specs,
        out_shape=out_shape,
        scratch_shapes=scratch,
        compiler_params=pltpu.CompilerParams(
            vmem_limit_bytes=(limit if whole else 56) * MIB
        ),
        cost_estimate=pl.CostEstimate(
            flops=flops // 1000, bytes_accessed=data // 1000, transcendentals=special // 1000
        ),
        name=name,
    )(*[value for value, _, _ in ins])


def fixed(value):
    return value, value.shape, lambda j: (0,) * value.ndim


def last(value, block):
    return value, value.shape[:-1] + (block,), lambda j: (0,) * (value.ndim - 1) + (j,)


def last_out(shape, dtype, block):
    return shape, dtype, shape[:-1] + (block,), lambda j: (0,) * (len(shape) - 1) + (j,)


def identity(size, order=lambda row: row):
    row = lax.broadcasted_iota(jnp.int32, (size, size), 0)
    column = lax.broadcasted_iota(jnp.int32, (size, size), 1)
    return (order(row) == column).astype(BF16)


def msa_kernel(msa_ref, cover_ref, left_w_ref, right_w_ref, right_ref, left_ref, values, rights, lefts):
    seqs, rows, breadth = msa_ref.shape
    proj = left_w_ref.shape[0]
    pairs = proj // 2
    tiles = breadth // LANES
    msa = msa_ref[...].astype(F32).reshape(seqs * rows, breadth)
    for tile in range(tiles):
        values[tile] = msa[:, tile * LANES : (tile + 1) * LANES]
    cover = cover_ref[...].astype(F32)
    swap = identity(proj, lambda row: 2 * (row % pairs) + row // pairs)
    right_w = jnp.dot(swap, right_w_ref[...], preferred_element_type=F32).astype(BF16)
    weights = jnp.concatenate([left_w_ref[...], right_w])
    for i in range(rows):
        row = jnp.concatenate(
            [values[tile, pl.ds(i, seqs, stride=rows), :] for tile in range(tiles)], axis=1
        )
        norm = standardize(row, -1).astype(BF16)
        factor = lax.dot_general(weights, norm, NT, preferred_element_type=F32)
        factor = factor * cover[i : i + 1]
        lefts[i] = factor[:proj]
        rights[i * pairs : (i + 1) * pairs] = jnp.concatenate(
            [factor[proj : proj + pairs], factor[proj + pairs :]], axis=1
        )
    half = rows // 2
    for i in range(half):
        left_ref[i * proj : (i + 1) * proj] = jnp.concatenate(
            [lefts[i], lefts[i + half]], axis=1
        ).astype(BF16)
    for t in range(pairs):
        right_ref[t] = rights[pl.ds(t, rows, stride=pairs), :].astype(BF16)
    right_ref[pairs] = jnp.concatenate([cover, jnp.zeros_like(cover)], axis=1).astype(BF16)


def msa_stage(msa, cover, left_w, right_w):
    seqs, rows, breadth = msa.shape
    proj = left_w.shape[0]
    right = (proj // 2 + 1, rows, 2 * seqs)
    left = (rows * proj // 2, 2 * seqs)
    return local_call(
        "msa_stage",
        msa_kernel,
        1,
        [fixed(msa), fixed(cover), fixed(left_w), fixed(right_w)],
        [(right, BF16, None, None), (left, BF16, None, None)],
        [
            pltpu.VMEM((breadth // LANES, seqs * rows, LANES), F32),
            pltpu.VMEM((rows * proj // 2, 2 * seqs), F32),
            pltpu.VMEM((rows, proj, seqs), F32),
        ],
        58,
        flops=4 * seqs * rows * breadth * proj,
        data=2 * seqs * rows * breadth,
        windows=True,
    )


def weights_kernel(
    mirror, out_ref, in_ref, gate_ref, final_ref, obs_ref, seen_ref, *refs
):
    out_t, in_t, gate_t, final_t, own_ref, far_ref, rows = refs
    one = identity(LANES)

    def turned(value):
        return lax.dot_general(one, value, NT, preferred_element_type=F32).astype(BF16)

    depth, width = out_ref.shape
    proj = int(depth**0.5)
    rows[...] = out_ref[...].astype(F32)
    ordered = jnp.concatenate([rows[pl.ds(q, proj, stride=proj), :] for q in range(proj)])
    out_t[...] = turned(ordered.astype(BF16))
    for k in range(in_ref.shape[1] // LANES):
        cols = slice(k * LANES, (k + 1) * LANES)
        in_t[cols] = turned(in_ref[:, cols])
    gate_t[...] = turned(gate_ref[...])
    final_t[...] = turned(final_ref[...])
    me = lax.axis_index("row")
    seen = seen_ref[...].astype(F32)
    for device, ref in ((me, own_ref), (mirror(me), far_ref)):
        for i in range(ref.shape[0]):
            ref[i : i + 1] = seen * obs_ref[device * ref.shape[0] + i].astype(F32)


def weights_stage(mirror, w_out, w_in, w_gate, w_final, obs, rows):
    depth, width = w_out.shape
    shapes = [w_out.shape[::-1], w_in.shape[::-1], w_gate.shape[::-1], w_final.shape[::-1]]
    return local_call(
        "weights_stage",
        lambda *refs: weights_kernel(mirror, *refs),
        1,
        [fixed(w_out), fixed(w_in), fixed(w_gate), fixed(w_final), scalars(obs)]
        + [fixed(obs[None])],
        [(shape, BF16, None, None) for shape in shapes]
        + [((rows,) + obs.shape, F32, None, None)] * 2,
        [pltpu.VMEM((depth, width), F32)],
        58,
        flops=2 * LANES * LANES * LANES * 6,
        data=4 * depth * width,
        windows=True,
    )


def order_right(right_refs, right):
    me = lax.axis_index("row")
    for index, ref in enumerate(right_refs):
        core, y = index // 2, index % 2
        for z in range(4):
            right[me ^ (4 * z + 2 * y + core)] = ref[z]


def make_updates(left_ref, mask, right, outer, scale):
    slices = right.shape[1]
    rows, depth, block = outer.shape
    proj = depth // (2 * (slices - 1))
    count = lax.dot_general(
        mask, right[:, slices - 1].reshape(block, LANES), NT, preferred_element_type=F32
    )
    scale[...] = 1.0 / jnp.maximum(count, 1.0)
    left = left_ref[...].astype(F32)
    turned = pltpu.roll(left, LANES // 2, 1)
    low = lax.broadcasted_iota(jnp.int32, left.shape, 1) < LANES // 2
    both_left = jnp.concatenate(
        [
            jnp.where(low, left, 0.0),
            jnp.where(low, turned, 0.0),
            jnp.where(low, 0.0, turned),
            jnp.where(low, 0.0, left),
        ]
    ).astype(BF16)
    half = rows * proj

    for t in range(slices - 1):
        both = lax.dot_general(
            both_left,
            right[:, t].reshape(block, LANES),
            NT,
            preferred_element_type=F32,
        ).astype(BF16)
        for e in range(2):
            outer[:, (2 * t + e) * proj : (2 * t + e + 1) * proj, :] = both[
                e * half : (e + 1) * half
            ].reshape(rows, proj, block)


def row_update(i, w_out_ref, outer, scale):
    update = jnp.dot(w_out_ref[...], outer[i], preferred_element_type=F32)
    return update * scale[i : i + 1]


def chip_here(split):
    return jnp.int32(0) if split == 1 else (lax.axis_index("row") // 2) & (split - 1)


def keep_sides(i, norm, w_in_ref, seen, sides_of, hidden):
    sides = jnp.dot(w_in_ref[...], norm, preferred_element_type=F32)
    stride = hidden + PAD
    for side, kept in enumerate(sides_of):
        gates = sides[2 * side * hidden : (2 * side + 1) * hidden]
        values = sides[(2 * side + 1) * hidden : (2 * side + 2) * hidden]
        value = sigmoid(gates) * values * seen
        for tile in range(kept.shape[0]):
            kept[tile, i * stride : i * stride + hidden] = value[
                :, tile * LANES : (tile + 1) * LANES
            ]


def write_sides(kept, outs, rows, hidden):
    per, chans = outs[0].shape[:2]
    chip = chip_here(len(outs))
    for part in range(per * len(outs)):
        target = outs[part // per].at[part % per]
        start = (chip ^ part) * chans

        @pl.loop(0, chans, unroll=8 if chans % 8 == 0 else chans)
        def _(c):
            for tile in range(kept.shape[0]):
                target[c, :, tile * LANES : (tile + 1) * LANES] = kept[
                    tile, pl.ds(start + c, rows, stride=hidden + PAD), :
                ].astype(BF16)


def pair_kernel(pieces, split, *refs):
    left_ref, mask_ref, couple_ref, w_out_ref, w_in_ref, seen_ref = refs[:6]
    right_refs, (pair_ref, *refs) = refs[6 : 6 + pieces], refs[6 + pieces :]
    a_refs, b_refs, refs = refs[:split], refs[split : 2 * split], refs[2 * split :]
    if pieces > 1:
        right, refs = refs[0], refs[1:]
        order_right(right_refs, right)
    else:
        right = right_refs[0]
    outer, kept_a, kept_b, scale = refs
    rows = couple_ref.shape[0]
    hidden = w_in_ref.shape[0] // 4
    make_updates(left_ref, mask_ref[...], right, outer, scale)
    for i in range(rows):
        pair = couple_ref[i].astype(F32).T + row_update(i, w_out_ref, outer, scale)
        norm = standardize(pair, 0).astype(BF16)
        pair_ref[i] = pair
        keep_sides(i, norm, w_in_ref, seen_ref[i : i + 1], (kept_a, kept_b), hidden)
    write_sides(kept_b, b_refs, rows, hidden)
    write_sides(kept_a, a_refs, rows, hidden)


def update_kernel(left_ref, w_out_ref, right, *refs):
    mask_refs, (update_ref, outer, scale) = refs[:-3], refs[-3:]
    if mask_refs:
        mask = mask_refs[0][...]
    else:
        mask = right[lax.axis_index("row") ^ 12, right.shape[1] - 1]
    make_updates(left_ref, mask, right, outer, scale)
    for i in range(update_ref.shape[0]):
        update_ref[i] = row_update(i, w_out_ref, outer, scale)


def mirror_kernel(update_ref, couple_ref, w_in_ref, seen_ref, *refs):
    outs, kept = refs[:-1], refs[-1]
    rows = couple_ref.shape[0]
    hidden = w_in_ref.shape[0] // 4
    for i in range(rows):
        pair = couple_ref[i].astype(F32).T + update_ref[i]
        norm = standardize(pair, 0).astype(BF16)
        keep_sides(i, norm, w_in_ref.at[2 * hidden :], seen_ref[i : i + 1], (kept,), hidden)
    write_sides(kept, outs, rows, hidden)


def right_input(value, total):
    return value, (value.shape[0] * BLOCK // total,) + value.shape[1:], lambda j: (j, 0, 0, 0)


def couple_input(couple):
    return couple, (couple.shape[0], BLOCK, couple.shape[2]), lambda j: (0, j, 0)


def kept_scratch(rows, hidden, block):
    return pltpu.VMEM((block // LANES, rows * (hidden + PAD), LANES), F32)


def scalars(value):
    return value, None, None


def pair_stage(left, right, mask, couple, w_out, w_in, seen, parts, split):
    rows, total, width = couple.shape
    hidden = w_in.shape[0] // 4
    piece = (parts // split, hidden // parts, rows, total)
    outs = [last_out((rows, width, total), F32, BLOCK)]
    outs += [last_out(piece, BF16, BLOCK)] * (2 * split)
    if len(right) > 1:
        outs += [((total // rows,) + right[0].shape[1:], BF16, None, None)]
    return local_call(
        "pair_stage",
        lambda *refs: pair_kernel(len(right), split, *refs),
        total // BLOCK,
        [fixed(left), fixed(mask), couple_input(couple), fixed(w_out), fixed(w_in)]
        + [last(seen, BLOCK)]
        + [right_input(value, total) for value in right],
        outs,
        [pltpu.VMEM((rows, w_out.shape[1], BLOCK), BF16)]
        + [kept_scratch(rows, hidden, BLOCK)] * 2
        + [pltpu.VMEM((rows, BLOCK), F32)],
        24,
        flops=4 * rows * total * w_out.shape[1] * width,
        data=16 * rows * total * width,
        special=2 * rows * total * hidden,
    )


def gate_kernel(pair_ref, w_gate_ref, gate_ref):
    for i in range(pair_ref.shape[0]):
        norm = standardize(pair_ref[i], 0).astype(BF16)
        gate_ref[i] = sigmoid(jnp.dot(w_gate_ref[...], norm, preferred_element_type=F32))


def gate_stage(pair, w_gate):
    rows, width, total = pair.shape
    return local_call(
        "gate_stage",
        gate_kernel,
        total // BLOCK,
        [last(pair, BLOCK), fixed(w_gate)],
        [last_out(pair.shape, F32, BLOCK)],
        [],
        16,
        flops=2 * rows * total * width * width,
        data=8 * rows * total * width,
        special=rows * total * width,
    )[0]


def update_stage(left, right, mask, w_out, rows, total):
    width = w_out.shape[0]
    return local_call(
        "update_stage",
        update_kernel,
        total // BLOCK,
        [fixed(left), fixed(w_out), right_input(right, total)]
        + ([] if mask is None else [fixed(mask)]),
        [last_out((rows, width, total), F32, BLOCK)],
        [pltpu.VMEM((rows, w_out.shape[1], BLOCK), BF16), pltpu.VMEM((rows, BLOCK), F32)],
        20,
        flops=4 * rows * total * w_out.shape[1] * width,
        data=8 * rows * total * width,
    )[0]


def mirror_stage(update, couple, w_in, seen, parts, split):
    rows, total, width = couple.shape
    hidden = w_in.shape[0] // 4
    return local_call(
        "mirror_stage",
        mirror_kernel,
        total // BLOCK,
        [last(update, BLOCK), couple_input(couple), fixed(w_in), last(seen, BLOCK)],
        [last_out((parts // split, hidden // parts, rows, total), BF16, BLOCK)] * split,
        [kept_scratch(rows, hidden, BLOCK)],
        16,
        flops=4 * rows * total * hidden * width,
        data=40000 * rows * total * width,
        special=rows * total * hidden,
    )


def tri_kernel(cores, split, flip, *refs):
    a_refs, refs = refs[:split], refs[split:]
    b_refs, refs = refs[: cores * split], refs[cores * split :]
    outs, whole = refs[:-1], refs[-1]
    per, chans, rows, total = a_refs[0].shape
    chip = chip_here(split)
    core = lax.axis_index("row") & 1
    for c in range(chans):
        for index, ref in enumerate(b_refs):
            for slot in range(per):
                part = (index % split) * per + slot
                place = (chip ^ part ^ flip) * cores
                if cores == 2:
                    place = place + (core ^ (index // split))
                whole[c, pl.ds(pl.multiple_of(place * rows, rows), rows), :] = ref[slot, c]
        side_a = jnp.concatenate([ref[slot, c] for ref in a_refs for slot in range(per)])
        product = lax.dot_general(side_a, whole[c], NT, preferred_element_type=F32).astype(BF16)
        for part in range(per * split):
            outs[part // per][part % per, c] = product[part * rows : (part + 1) * rows]


def channels(value, step):
    return value, value.shape[:1] + (step,) + value.shape[2:], lambda c: (0, c, 0, 0)


def tri_stage(a, b, cores, flip):
    split = len(a)
    per, chans, rows, total = a[0].shape
    step = max(1, min(chans, chans * BLOCK // total))
    half = per * split * cores * rows
    shape = (per, chans, rows, half)
    return local_call(
        "tri_stage",
        lambda *refs: tri_kernel(cores, split, flip, *refs),
        chans // step,
        [channels(value, step) for value in a]
        + [channels(value, step) for value in b],
        [(shape, BF16, (per, step, rows, half), lambda c: (0, c, 0, 0))] * split,
        [pltpu.VMEM((step, half, total), BF16)],
        16,
        flops=2 * chans * per * split * rows * half * total,
        data=6 * chans * half * total,
    )


def final_rows(tri, low, pair_ref, gate_ref, w_ref, normed, write):
    rows = pair_ref.shape[0]
    per, chans, _, block = tri[0].shape
    parts = per * len(tri)
    hidden = chans * parts
    tiles = block // LANES
    chip = chip_here(len(tri))
    values = standardize(
        jnp.concatenate([ref[slot] for ref in tri for slot in range(per)]).astype(F32), 0
    )
    for part in range(parts):
        first = pl.multiple_of((chip ^ part) * (chans * rows), chans * rows)
        for tile in range(tiles):
            normed[tile, pl.ds(first, chans * rows), :] = values[
                part * chans : (part + 1) * chans, :, tile * LANES : (tile + 1) * LANES
            ].reshape(chans * rows, LANES)
    for i in range(rows):
        columns = jnp.concatenate(
            [normed[tile, pl.ds(i, hidden, stride=rows), :] for tile in range(tiles)], axis=1
        ).astype(BF16)
        update = jnp.dot(w_ref[...], columns, preferred_element_type=F32)
        cols = pl.ds(low, block)
        result = pair_ref[i, :, cols] + gate_ref[i, :, cols] * update
        write(i, result.T.astype(BF16))


def half_start(far, block):
    mine = lax.div(lax.axis_index("row"), lax.axis_size("row") // 2)
    return pl.multiple_of((mine ^ far) * block, block)


def near_kernel(pair_ref, gate_ref, w_ref, *refs):
    tri, (out_ref, normed) = refs[:-2], refs[-2:]

    def write(i, result):
        out_ref[i] = result

    low = half_start(0, tri[0].shape[-1])
    final_rows(tri, low, pair_ref, gate_ref, w_ref, normed, write)


def near_stage(tri, pair, gate, weight):
    rows, width, _ = pair.shape
    hidden, block = weight.shape[1], tri[0].shape[-1]
    return local_call(
        "near_stage",
        near_kernel,
        1,
        [fixed(pair), fixed(gate), fixed(weight)] + [fixed(value) for value in tri],
        [((rows, block, width), BF16, None, None)],
        [pltpu.VMEM((block // LANES, hidden * rows, LANES), F32)],
        16,
        flops=2 * rows * block * hidden * width,
        data=12 * rows * block * width,
    )[0]


def final_kernel(split, pair_ref, gate_ref, w_ref, *refs):
    out_ref, normed = refs[-2:]
    tri, near = refs[:split], refs[split:-2]
    block = tri[0].shape[-1]
    low = half_start(1, block) if near else 0

    def write(i, result):
        out_ref[i, pl.ds(low, block), :] = result
        if near:
            out_ref[i, pl.ds(half_start(0, block), block), :] = near[0][i]

    final_rows(tri, low, pair_ref, gate_ref, w_ref, normed, write)


def final_stage(tri, near, pair, gate, weight):
    rows, width, total = pair.shape
    hidden, split = weight.shape[1], len(tri)
    block = BLOCK if near is None else tri[0].shape[-1]
    return local_call(
        "final_stage",
        lambda *refs: final_kernel(split, *refs),
        total // BLOCK,
        [last(pair, BLOCK), last(gate, BLOCK), fixed(weight)]
        + [last(value, block) for value in tri]
        + ([] if near is None else [fixed(near)]),
        [((rows, total, width), BF16, (rows, BLOCK, width), lambda j: (0, j, 0))],
        [pltpu.VMEM((block // LANES, hidden * rows, LANES), F32)],
        24,
        flops=2 * rows * total * hidden * width,
        data=12 * rows * total * width,
    )[0]


def send(value, move):
    devs = lax.axis_size("row")
    return lax.ppermute(value, "row", [(i, move(i)) for i in range(devs)])


def after(first, value):
    return lax.optimization_barrier((first, value))


def exchange(pieces, earlier=None):
    devs = lax.axis_size("row")
    half = devs // 2
    if len(pieces) == 1:
        groups = [list(range(half)), list(range(half, devs))]
        return [
            lax.all_to_all(
                pieces[0], "row", split_axis=0, concat_axis=0, tiled=True, axis_index_groups=groups
            )
        ]
    out = list(pieces)
    for r in range(1, len(out)):
        if earlier is not None:
            _, out[r] = after(earlier[r], out[r])
        out[r] = send(out[r], lambda i, r=r: i ^ (2 * r))
    return out


def with_other_core(pieces):
    if len(pieces) == 1:
        return pieces
    return list(pieces) + [send(value, lambda i: i ^ 1) for value in pieces]


def body(
    homolog_features,
    coverage_indicator,
    couple_features,
    observed_indicator,
    first_factor_matrix,
    second_factor_matrix,
    product_final_matrix,
    edge_projection_matrix,
    sigmoid_filter_matrix,
    multiplicative_final_matrix,
):
    rows, total, width = couple_features.shape
    devs = lax.axis_size("row")
    half = devs // 2
    me = lax.axis_index("row")
    hops = devs == 16
    cores = 2 if hops else 1
    parts = half // cores
    split = parts if hops else 1

    def mirror(device):
        return device ^ 12 if hops else (device + half) % devs

    def mirrored(value):
        return send(value, mirror)

    block, left = msa_stage(
        homolog_features,
        coverage_indicator.T,
        first_factor_matrix.T,
        second_factor_matrix.T,
    )
    weights = weights_stage(
        mirror,
        product_final_matrix,
        edge_projection_matrix,
        sigmoid_filter_matrix,
        multiplicative_final_matrix,
        observed_indicator,
        rows,
    )
    if hops:
        slices = block.shape[0]
        both = send(jnp.concatenate([block, left.reshape((-1,) + block.shape[1:])]), mirror)
        held = [block, send(block, lambda i: i ^ 4), send(block, lambda i: i ^ 8), both[:slices]]
        far_left = both[slices:].reshape(left.shape)
        held, (couple_out, weights) = after(jnp.stack(held), (couple_features, weights))
        far_couple = mirrored(couple_out)
        other = send(held, lambda i: i ^ 2)
        right = [held, other, send(held, lambda i: i ^ 1), send(other, lambda i: i ^ 1)]
        far_mask = None
    else:
        right = [lax.all_gather(block, "row", axis=0)]
        far_left = mirrored(left)
        far_couple = mirrored(couple_features)
        far_mask = right[0][mirror(me), -1]
    w_out, w_in, w_gate, w_final, seen, far_seen = weights

    pair, *sides = pair_stage(
        left, right, block[-1], couple_features, w_out, w_in, seen, parts, split
    )
    a, b = list(sides[:split]), list(sides[split : 2 * split])
    ordered = sides[2 * split] if hops else right[0]
    b = exchange(b)
    if hops:
        _, far_left = after(b[1], far_left)
    update = update_stage(far_left, ordered, far_mask, w_out, rows, total)
    if hops:
        update, a[2] = after(update, a[2])
    a = exchange(a, b)
    near = tri_stage(a, with_other_core(b), cores, 0)
    far_b = mirror_stage(update, far_couple, w_in, far_seen, parts, split)
    far_b = exchange(far_b, a)
    if hops:
        near, pair = after(near, pair)
    gate = gate_stage(pair, w_gate)
    if hops:
        (near, gate), far_b = after((near, gate), far_b)
    near = exchange(near)
    far = exchange(tri_stage(a, with_other_core(far_b), cores, 2 if hops else 0))
    if hops:
        done = near_stage(near, pair, gate, w_final)
        return final_stage(far, done, pair, gate, w_final)
    lower = me < half
    tri = [
        jnp.concatenate([jnp.where(lower, x, y), jnp.where(lower, y, x)], axis=-1)
        for x, y in zip(near, far)
    ]
    return final_stage(tri, None, pair, gate, w_final)


def solution(mesh):
    placed = (
        P(None, ("groups", "row"), None),
        P(None, ("groups", "row")),
        P(("groups", "row"), None, None),
        P("groups"),
        P(),
        P(),
        P(),
        P(),
        P(),
        P(),
    )
    return jax.shard_map(
        body,
        mesh=mesh,
        in_specs=placed,
        out_specs=P(("groups", "row"), None, None),
        check_vma=False,
    )
```

```python
import jax
import jax.numpy as jnp
from jax import lax
from jax.experimental import pallas as pl
from jax.experimental.pallas import tpu as pltpu
from jax.sharding import PartitionSpec as P

F32 = jnp.float32
BF16 = jnp.bfloat16
LANES = 128
BLOCK = 2 * LANES
PAD = 8
NT = (((1,), (1,)), ((), ()))
MIB = 1024 * 1024


def sigmoid(value):
    return 0.5 * jnp.tanh(0.5 * value) + 0.5


def standardize(value, axis):
    mean = jnp.mean(value, axis=axis, keepdims=True)
    centred = value - mean
    var = jnp.mean(centred * centred, axis=axis, keepdims=True)
    return centred * lax.rsqrt(var + 1e-05)


def local_call(name, kernel, steps, ins, outs, scratch, limit, flops=0, data=0, special=0, windows=False):
    whole = steps == 1
    in_specs, out_specs, out_shape = [], [], []
    for value, block, index in ins:
        if block is None:
            in_specs.append(pl.BlockSpec(memory_space=pltpu.SMEM))
        elif whole and windows:
            in_specs.append(pl.BlockSpec(value.shape, lambda ndim=value.ndim: (0,) * ndim))
        elif whole:
            in_specs.append(pl.BlockSpec(memory_space=pltpu.VMEM))
        else:
            in_specs.append(pl.BlockSpec(block, index))
    for shape, dtype, block, index in outs:
        if whole:
            out_specs.append(pl.BlockSpec(memory_space=pltpu.VMEM))
        else:
            out_specs.append(pl.BlockSpec(block, index))
        keep = whole and name != "final_stage"
        out_shape.append(
            pltpu.VMEM(shape, dtype) if keep else jax.ShapeDtypeStruct(shape, dtype)
        )
    return pl.pallas_call(
        kernel,
        grid=() if whole else (steps,),
        in_specs=in_specs,
        out_specs=out_specs,
        out_shape=out_shape,
        scratch_shapes=scratch,
        compiler_params=pltpu.CompilerParams(
            vmem_limit_bytes=(limit if whole else 56) * MIB
        ),
        cost_estimate=pl.CostEstimate(
            flops=flops // 1000, bytes_accessed=data // 1000, transcendentals=special // 1000
        ),
        name=name,
    )(*[value for value, _, _ in ins])


def fixed(value):
    return value, value.shape, lambda j: (0,) * value.ndim


def last(value, block):
    return value, value.shape[:-1] + (block,), lambda j: (0,) * (value.ndim - 1) + (j,)


def last_out(shape, dtype, block):
    return shape, dtype, shape[:-1] + (block,), lambda j: (0,) * (len(shape) - 1) + (j,)


def identity(size, order=lambda row: row):
    row = lax.broadcasted_iota(jnp.int32, (size, size), 0)
    column = lax.broadcasted_iota(jnp.int32, (size, size), 1)
    return (order(row) == column).astype(BF16)


def msa_kernel(msa_ref, cover_ref, left_w_ref, right_w_ref, right_ref, left_ref, values, rights, lefts):
    seqs, rows, breadth = msa_ref.shape
    proj = left_w_ref.shape[0]
    pairs = proj // 2
    tiles = breadth // LANES
    msa = msa_ref[...].astype(F32).reshape(seqs * rows, breadth)
    for tile in range(tiles):
        values[tile] = msa[:, tile * LANES : (tile + 1) * LANES]
    cover = cover_ref[...].astype(F32)
    swap = identity(proj, lambda row: 2 * (row % pairs) + row // pairs)
    right_w = jnp.dot(swap, right_w_ref[...], preferred_element_type=F32).astype(BF16)
    weights = jnp.concatenate([left_w_ref[...], right_w])
    for i in range(rows):
        row = jnp.concatenate(
            [values[tile, pl.ds(i, seqs, stride=rows), :] for tile in range(tiles)], axis=1
        )
        norm = standardize(row, -1).astype(BF16)
        factor = lax.dot_general(weights, norm, NT, preferred_element_type=F32)
        factor = factor * cover[i : i + 1]
        lefts[i] = factor[:proj]
        rights[i * pairs : (i + 1) * pairs] = jnp.concatenate(
            [factor[proj : proj + pairs], factor[proj + pairs :]], axis=1
        )
    half = rows // 2
    for i in range(half):
        left_ref[i * proj : (i + 1) * proj] = jnp.concatenate(
            [lefts[i], lefts[i + half]], axis=1
        ).astype(BF16)
    for t in range(pairs):
        right_ref[t] = rights[pl.ds(t, rows, stride=pairs), :].astype(BF16)
    right_ref[pairs] = jnp.concatenate([cover, jnp.zeros_like(cover)], axis=1).astype(BF16)


def msa_stage(msa, cover, left_w, right_w):
    seqs, rows, breadth = msa.shape
    proj = left_w.shape[0]
    right = (proj // 2 + 1, rows, 2 * seqs)
    left = (rows * proj // 2, 2 * seqs)
    return local_call(
        "msa_stage",
        msa_kernel,
        1,
        [fixed(msa), fixed(cover), fixed(left_w), fixed(right_w)],
        [(right, BF16, None, None), (left, BF16, None, None)],
        [
            pltpu.VMEM((breadth // LANES, seqs * rows, LANES), F32),
            pltpu.VMEM((rows * proj // 2, 2 * seqs), F32),
            pltpu.VMEM((rows, proj, seqs), F32),
        ],
        58,
        flops=4 * seqs * rows * breadth * proj,
        data=2 * seqs * rows * breadth,
        windows=True,
    )


def weights_kernel(
    mirror, out_ref, in_ref, gate_ref, final_ref, obs_ref, seen_ref, *refs
):
    out_t, in_t, gate_t, final_t, own_ref, far_ref, rows = refs
    one = identity(LANES)

    def turned(value):
        return lax.dot_general(one, value, NT, preferred_element_type=F32).astype(BF16)

    depth, width = out_ref.shape
    proj = int(depth**0.5)
    rows[...] = out_ref[...].astype(F32)
    ordered = jnp.concatenate([rows[pl.ds(q, proj, stride=proj), :] for q in range(proj)])
    out_t[...] = turned(ordered.astype(BF16))
    for k in range(in_ref.shape[1] // LANES):
        cols = slice(k * LANES, (k + 1) * LANES)
        in_t[cols] = turned(in_ref[:, cols])
    gate_t[...] = turned(gate_ref[...])
    final_t[...] = turned(final_ref[...])
    me = lax.axis_index("row")
    seen = seen_ref[...].astype(F32)
    for device, ref in ((me, own_ref), (mirror(me), far_ref)):
        for i in range(ref.shape[0]):
            ref[i : i + 1] = seen * obs_ref[device * ref.shape[0] + i].astype(F32)


def weights_stage(mirror, w_out, w_in, w_gate, w_final, obs, rows):
    depth, width = w_out.shape
    shapes = [w_out.shape[::-1], w_in.shape[::-1], w_gate.shape[::-1], w_final.shape[::-1]]
    return local_call(
        "weights_stage",
        lambda *refs: weights_kernel(mirror, *refs),
        1,
        [fixed(w_out), fixed(w_in), fixed(w_gate), fixed(w_final), scalars(obs)]
        + [fixed(obs[None])],
        [(shape, BF16, None, None) for shape in shapes]
        + [((rows,) + obs.shape, F32, None, None)] * 2,
        [pltpu.VMEM((depth, width), F32)],
        58,
        flops=2 * LANES * LANES * LANES * 6,
        data=4 * depth * width,
        windows=True,
    )


def order_right(right_refs, right):
    me = lax.axis_index("row")
    for index, ref in enumerate(right_refs):
        core, y = index // 2, index % 2
        for z in range(4):
            right[me ^ (4 * z + 2 * y + core)] = ref[z]


def make_updates(left_ref, mask, right, outer, scale):
    slices = right.shape[1]
    rows, depth, block = outer.shape
    proj = depth // (2 * (slices - 1))
    count = lax.dot_general(
        mask, right[:, slices - 1].reshape(block, LANES), NT, preferred_element_type=F32
    )
    scale[...] = 1.0 / jnp.maximum(count, 1.0)
    left = left_ref[...].astype(F32)
    turned = pltpu.roll(left, LANES // 2, 1)
    low = lax.broadcasted_iota(jnp.int32, left.shape, 1) < LANES // 2
    both_left = jnp.concatenate(
        [
            jnp.where(low, left, 0.0),
            jnp.where(low, turned, 0.0),
            jnp.where(low, 0.0, turned),
            jnp.where(low, 0.0, left),
        ]
    ).astype(BF16)
    half = rows * proj

    for t in range(slices - 1):
        both = lax.dot_general(
            both_left,
            right[:, t].reshape(block, LANES),
            NT,
            preferred_element_type=F32,
        ).astype(BF16)
        for e in range(2):
            outer[:, (2 * t + e) * proj : (2 * t + e + 1) * proj, :] = both[
                e * half : (e + 1) * half
            ].reshape(rows, proj, block)


def row_update(i, w_out_ref, outer, scale):
    update = jnp.dot(w_out_ref[...], outer[i], preferred_element_type=F32)
    return update * scale[i : i + 1]


def chip_here(split):
    return jnp.int32(0) if split == 1 else (lax.axis_index("row") // 2) & (split - 1)


def keep_sides(i, norm, w_in_ref, seen, sides_of, hidden):
    sides = jnp.dot(w_in_ref[...], norm, preferred_element_type=F32)
    stride = hidden + PAD
    for side, kept in enumerate(sides_of):
        gates = sides[2 * side * hidden : (2 * side + 1) * hidden]
        values = sides[(2 * side + 1) * hidden : (2 * side + 2) * hidden]
        value = sigmoid(gates) * values * seen
        for tile in range(kept.shape[0]):
            kept[tile, i * stride : i * stride + hidden] = value[
                :, tile * LANES : (tile + 1) * LANES
            ]


def write_sides(kept, outs, rows, hidden):
    per, chans = outs[0].shape[:2]
    chip = chip_here(len(outs))
    for part in range(per * len(outs)):
        target = outs[part // per].at[part % per]
        start = (chip ^ part) * chans

        @pl.loop(0, chans, unroll=8 if chans % 8 == 0 else chans)
        def _(c):
            for tile in range(kept.shape[0]):
                target[c, :, tile * LANES : (tile + 1) * LANES] = kept[
                    tile, pl.ds(start + c, rows, stride=hidden + PAD), :
                ].astype(BF16)


def pair_kernel(pieces, split, *refs):
    left_ref, mask_ref, couple_ref, w_out_ref, w_in_ref, seen_ref = refs[:6]
    right_refs, (pair_ref, *refs) = refs[6 : 6 + pieces], refs[6 + pieces :]
    a_refs, b_refs, refs = refs[:split], refs[split : 2 * split], refs[2 * split :]
    if pieces > 1:
        right, refs = refs[0], refs[1:]
        order_right(right_refs, right)
    else:
        right = right_refs[0]
    outer, kept_a, kept_b, scale = refs
    rows = couple_ref.shape[0]
    hidden = w_in_ref.shape[0] // 4
    make_updates(left_ref, mask_ref[...], right, outer, scale)
    for i in range(rows):
        pair = couple_ref[i].astype(F32).T + row_update(i, w_out_ref, outer, scale)
        norm = standardize(pair, 0).astype(BF16)
        pair_ref[i] = pair
        keep_sides(i, norm, w_in_ref, seen_ref[i : i + 1], (kept_a, kept_b), hidden)
    write_sides(kept_b, b_refs, rows, hidden)
    write_sides(kept_a, a_refs, rows, hidden)


def update_kernel(left_ref, w_out_ref, right, *refs):
    mask_refs, (update_ref, outer, scale) = refs[:-3], refs[-3:]
    if mask_refs:
        mask = mask_refs[0][...]
    else:
        mask = right[lax.axis_index("row") ^ 12, right.shape[1] - 1]
    make_updates(left_ref, mask, right, outer, scale)
    for i in range(update_ref.shape[0]):
        update_ref[i] = row_update(i, w_out_ref, outer, scale)


def mirror_kernel(update_ref, couple_ref, w_in_ref, seen_ref, *refs):
    outs, kept = refs[:-1], refs[-1]
    rows = couple_ref.shape[0]
    hidden = w_in_ref.shape[0] // 4
    for i in range(rows):
        pair = couple_ref[i].astype(F32).T + update_ref[i]
        norm = standardize(pair, 0).astype(BF16)
        keep_sides(i, norm, w_in_ref.at[2 * hidden :], seen_ref[i : i + 1], (kept,), hidden)
    write_sides(kept, outs, rows, hidden)


def right_input(value, total):
    return value, (value.shape[0] * BLOCK // total,) + value.shape[1:], lambda j: (j, 0, 0, 0)


def couple_input(couple):
    return couple, (couple.shape[0], BLOCK, couple.shape[2]), lambda j: (0, j, 0)


def kept_scratch(rows, hidden, block):
    return pltpu.VMEM((block // LANES, rows * (hidden + PAD), LANES), F32)


def scalars(value):
    return value, None, None


def pair_stage(left, right, mask, couple, w_out, w_in, seen, parts, split):
    rows, total, width = couple.shape
    hidden = w_in.shape[0] // 4
    piece = (parts // split, hidden // parts, rows, total)
    outs = [last_out((rows, width, total), F32, BLOCK)]
    outs += [last_out(piece, BF16, BLOCK)] * (2 * split)
    if len(right) > 1:
        outs += [((total // rows,) + right[0].shape[1:], BF16, None, None)]
    return local_call(
        "pair_stage",
        lambda *refs: pair_kernel(len(right), split, *refs),
        total // BLOCK,
        [fixed(left), fixed(mask), couple_input(couple), fixed(w_out), fixed(w_in)]
        + [last(seen, BLOCK)]
        + [right_input(value, total) for value in right],
        outs,
        [pltpu.VMEM((rows, w_out.shape[1], BLOCK), BF16)]
        + [kept_scratch(rows, hidden, BLOCK)] * 2
        + [pltpu.VMEM((rows, BLOCK), F32)],
        24,
        flops=4 * rows * total * w_out.shape[1] * width,
        data=16 * rows * total * width,
        special=2 * rows * total * hidden,
    )


def gate_kernel(pair_ref, w_gate_ref, gate_ref):
    for i in range(pair_ref.shape[0]):
        norm = standardize(pair_ref[i], 0).astype(BF16)
        gate_ref[i] = sigmoid(jnp.dot(w_gate_ref[...], norm, preferred_element_type=F32))


def gate_stage(pair, w_gate):
    rows, width, total = pair.shape
    return local_call(
        "gate_stage",
        gate_kernel,
        total // BLOCK,
        [last(pair, BLOCK), fixed(w_gate)],
        [last_out(pair.shape, F32, BLOCK)],
        [],
        16,
        flops=2 * rows * total * width * width,
        data=8 * rows * total * width,
        special=rows * total * width,
    )[0]


def update_stage(left, right, mask, w_out, rows, total):
    width = w_out.shape[0]
    return local_call(
        "update_stage",
        update_kernel,
        total // BLOCK,
        [fixed(left), fixed(w_out), right_input(right, total)]
        + ([] if mask is None else [fixed(mask)]),
        [last_out((rows, width, total), F32, BLOCK)],
        [pltpu.VMEM((rows, w_out.shape[1], BLOCK), BF16), pltpu.VMEM((rows, BLOCK), F32)],
        20,
        flops=4 * rows * total * w_out.shape[1] * width,
        data=8 * rows * total * width,
    )[0]


def mirror_stage(update, couple, w_in, seen, parts, split):
    rows, total, width = couple.shape
    hidden = w_in.shape[0] // 4
    return local_call(
        "mirror_stage",
        mirror_kernel,
        total // BLOCK,
        [last(update, BLOCK), couple_input(couple), fixed(w_in), last(seen, BLOCK)],
        [last_out((parts // split, hidden // parts, rows, total), BF16, BLOCK)] * split,
        [kept_scratch(rows, hidden, BLOCK)],
        16,
        flops=4 * rows * total * hidden * width,
        data=40000 * rows * total * width,
        special=rows * total * hidden,
    )


def tri_kernel(cores, split, flip, *refs):
    a_refs, refs = refs[:split], refs[split:]
    b_refs, refs = refs[: cores * split], refs[cores * split :]
    outs, whole = refs[:-1], refs[-1]
    per, chans, rows, total = a_refs[0].shape
    chip = chip_here(split)
    core = lax.axis_index("row") & 1
    for c in range(chans):
        for index, ref in enumerate(b_refs):
            for slot in range(per):
                part = (index % split) * per + slot
                place = (chip ^ part ^ flip) * cores
                if cores == 2:
                    place = place + (core ^ (index // split))
                whole[c, pl.ds(pl.multiple_of(place * rows, rows), rows), :] = ref[slot, c]
        side_a = jnp.concatenate([ref[slot, c] for ref in a_refs for slot in range(per)])
        product = lax.dot_general(side_a, whole[c], NT, preferred_element_type=F32).astype(BF16)
        for part in range(per * split):
            outs[part // per][part % per, c] = product[part * rows : (part + 1) * rows]


def channels(value, step):
    return value, value.shape[:1] + (step,) + value.shape[2:], lambda c: (0, c, 0, 0)


def tri_stage(a, b, cores, flip):
    split = len(a)
    per, chans, rows, total = a[0].shape
    step = max(1, min(chans, chans * BLOCK // total))
    half = per * split * cores * rows
    shape = (per, chans, rows, half)
    return local_call(
        "tri_stage",
        lambda *refs: tri_kernel(cores, split, flip, *refs),
        chans // step,
        [channels(value, step) for value in a]
        + [channels(value, step) for value in b],
        [(shape, BF16, (per, step, rows, half), lambda c: (0, c, 0, 0))] * split,
        [pltpu.VMEM((step, half, total), BF16)],
        16,
        flops=2 * chans * per * split * rows * half * total,
        data=6 * chans * half * total,
    )


def final_rows(tri, low, pair_ref, gate_ref, w_ref, normed, write):
    rows = pair_ref.shape[0]
    per, chans, _, block = tri[0].shape
    parts = per * len(tri)
    hidden = chans * parts
    tiles = block // LANES
    chip = chip_here(len(tri))
    values = standardize(
        jnp.concatenate([ref[slot] for ref in tri for slot in range(per)]).astype(F32), 0
    )
    for part in range(parts):
        first = pl.multiple_of((chip ^ part) * (chans * rows), chans * rows)
        for tile in range(tiles):
            normed[tile, pl.ds(first, chans * rows), :] = values[
                part * chans : (part + 1) * chans, :, tile * LANES : (tile + 1) * LANES
            ].reshape(chans * rows, LANES)
    for i in range(rows):
        columns = jnp.concatenate(
            [normed[tile, pl.ds(i, hidden, stride=rows), :] for tile in range(tiles)], axis=1
        ).astype(BF16)
        update = jnp.dot(w_ref[...], columns, preferred_element_type=F32)
        cols = pl.ds(low, block)
        result = pair_ref[i, :, cols] + gate_ref[i, :, cols] * update
        write(i, result.T.astype(BF16))


def half_start(far, block):
    mine = lax.div(lax.axis_index("row"), lax.axis_size("row") // 2)
    return pl.multiple_of((mine ^ far) * block, block)


def near_kernel(pair_ref, gate_ref, w_ref, *refs):
    tri, (out_ref, normed) = refs[:-2], refs[-2:]

    def write(i, result):
        out_ref[i] = result

    low = half_start(0, tri[0].shape[-1])
    final_rows(tri, low, pair_ref, gate_ref, w_ref, normed, write)


def near_stage(tri, pair, gate, weight):
    rows, width, _ = pair.shape
    hidden, block = weight.shape[1], tri[0].shape[-1]
    return local_call(
        "near_stage",
        near_kernel,
        1,
        [fixed(pair), fixed(gate), fixed(weight)] + [fixed(value) for value in tri],
        [((rows, block, width), BF16, None, None)],
        [pltpu.VMEM((block // LANES, hidden * rows, LANES), F32)],
        16,
        flops=2 * rows * block * hidden * width,
        data=12 * rows * block * width,
    )[0]


def final_kernel(split, pair_ref, gate_ref, w_ref, *refs):
    out_ref, normed = refs[-2:]
    tri, near = refs[:split], refs[split:-2]
    block = tri[0].shape[-1]
    low = half_start(1, block) if near else 0

    def write(i, result):
        out_ref[i, pl.ds(low, block), :] = result
        if near:
            out_ref[i, pl.ds(half_start(0, block), block), :] = near[0][i]

    final_rows(tri, low, pair_ref, gate_ref, w_ref, normed, write)


def final_stage(tri, near, pair, gate, weight):
    rows, width, total = pair.shape
    hidden, split = weight.shape[1], len(tri)
    block = BLOCK if near is None else tri[0].shape[-1]
    return local_call(
        "final_stage",
        lambda *refs: final_kernel(split, *refs),
        total // BLOCK,
        [last(pair, BLOCK), last(gate, BLOCK), fixed(weight)]
        + [last(value, block) for value in tri]
        + ([] if near is None else [fixed(near)]),
        [((rows, total, width), BF16, (rows, BLOCK, width), lambda j: (0, j, 0))],
        [pltpu.VMEM((block // LANES, hidden * rows, LANES), F32)],
        24,
        flops=2 * rows * total * hidden * width,
        data=12 * rows * total * width,
    )[0]


def send(value, move):
    devs = lax.axis_size("row")
    return lax.ppermute(value, "row", [(i, move(i)) for i in range(devs)])


def after(first, value):
    return lax.optimization_barrier((first, value))


def exchange(pieces, earlier=None):
    devs = lax.axis_size("row")
    half = devs // 2
    if len(pieces) == 1:
        groups = [list(range(half)), list(range(half, devs))]
        return [
            lax.all_to_all(
                pieces[0], "row", split_axis=0, concat_axis=0, tiled=True, axis_index_groups=groups
            )
        ]
    out = list(pieces)
    for r in range(1, len(out)):
        if earlier is not None:
            _, out[r] = after(earlier[r], out[r])
        out[r] = send(out[r], lambda i, r=r: i ^ (2 * r))
    return out


def with_other_core(pieces):
    if len(pieces) == 1:
        return pieces
    return list(pieces) + [send(value, lambda i: i ^ 1) for value in pieces]


def body(
    homolog_features,
    coverage_indicator,
    couple_features,
    observed_indicator,
    first_factor_matrix,
    second_factor_matrix,
    product_final_matrix,
    edge_projection_matrix,
    sigmoid_filter_matrix,
    multiplicative_final_matrix,
):
    rows, total, width = couple_features.shape
    devs = lax.axis_size("row")
    half = devs // 2
    me = lax.axis_index("row")
    hops = devs == 16
    cores = 2 if hops else 1
    parts = half // cores
    split = parts if hops else 1

    def mirror(device):
        return device ^ 12 if hops else (device + half) % devs

    def mirrored(value):
        return send(value, mirror)

    block, left = msa_stage(
        homolog_features,
        coverage_indicator.T,
        first_factor_matrix.T,
        second_factor_matrix.T,
    )
    weights = weights_stage(
        mirror,
        product_final_matrix,
        edge_projection_matrix,
        sigmoid_filter_matrix,
        multiplicative_final_matrix,
        observed_indicator,
        rows,
    )
    if hops:
        slices = block.shape[0]
        both = send(jnp.concatenate([block, left.reshape((-1,) + block.shape[1:])]), mirror)
        held = [block, send(block, lambda i: i ^ 4), send(block, lambda i: i ^ 8), both[:slices]]
        far_left = both[slices:].reshape(left.shape)
        held, (couple_out, weights) = after(jnp.stack(held), (couple_features, weights))
        far_couple = mirrored(couple_out)
        other = send(held, lambda i: i ^ 2)
        right = [held, other, send(held, lambda i: i ^ 1), send(other, lambda i: i ^ 1)]
        far_mask = None
    else:
        right = [lax.all_gather(block, "row", axis=0)]
        far_left = mirrored(left)
        far_couple = mirrored(couple_features)
        far_mask = right[0][mirror(me), -1]
    w_out, w_in, w_gate, w_final, seen, far_seen = weights

    pair, *sides = pair_stage(
        left, right, block[-1], couple_features, w_out, w_in, seen, parts, split
    )
    a, b = list(sides[:split]), list(sides[split : 2 * split])
    ordered = sides[2 * split] if hops else right[0]
    b = exchange(b)
    if hops:
        _, far_left = after(b[1], far_left)
    update = update_stage(far_left, ordered, far_mask, w_out, rows, total)
    if hops:
        update, a[2] = after(update, a[2])
    a = exchange(a, b)
    near = tri_stage(a, with_other_core(b), cores, 0)
    far_b = mirror_stage(update, far_couple, w_in, far_seen, parts, split)
    if hops:
        far_b = list(far_b)
        _, far_b[1] = after(a[3], far_b[1])
        _, far_b[2:] = after(a[1], far_b[2:])
    far_b = exchange(far_b)
    if hops:
        near, pair = after(near, pair)
    gate = gate_stage(pair, w_gate)
    if hops:
        (near, gate), far_b = after((near, gate), far_b)
    near = exchange(near)
    far = exchange(tri_stage(a, with_other_core(far_b), cores, 2 if hops else 0))
    if hops:
        done = near_stage(near, pair, gate, w_final)
        return final_stage(far, done, pair, gate, w_final)
    lower = me < half
    tri = [
        jnp.concatenate([jnp.where(lower, x, y), jnp.where(lower, y, x)], axis=-1)
        for x, y in zip(near, far)
    ]
    return final_stage(tri, None, pair, gate, w_final)


def solution(mesh):
    placed = (
        P(None, ("groups", "row"), None),
        P(None, ("groups", "row")),
        P(("groups", "row"), None, None),
        P("groups"),
        P(),
        P(),
        P(),
        P(),
        P(),
        P(),
    )
    return jax.shard_map(
        body,
        mesh=mesh,
        in_specs=placed,
        out_specs=P(("groups", "row"), None, None),
        check_vma=False,
    )
```

```python
import jax
import jax.numpy as jnp
from jax import lax
from jax.experimental import pallas as pl
from jax.experimental.pallas import tpu as pltpu
from jax.sharding import PartitionSpec as P

F32 = jnp.float32
BF16 = jnp.bfloat16
LANES = 128
BLOCK = 2 * LANES
PAD = 8
NT = (((1,), (1,)), ((), ()))
MIB = 1024 * 1024


def sigmoid(value):
    return 0.5 * jnp.tanh(0.5 * value) + 0.5


def standardize(value, axis):
    mean = jnp.mean(value, axis=axis, keepdims=True)
    centred = value - mean
    var = jnp.mean(centred * centred, axis=axis, keepdims=True)
    return centred * lax.rsqrt(var + 1e-05)


def local_call(name, kernel, steps, ins, outs, scratch, limit, flops=0, data=0, special=0, windows=False):
    whole = steps == 1
    in_specs, out_specs, out_shape = [], [], []
    for value, block, index in ins:
        if block is None:
            in_specs.append(pl.BlockSpec(memory_space=pltpu.SMEM))
        elif whole and windows:
            in_specs.append(pl.BlockSpec(value.shape, lambda ndim=value.ndim: (0,) * ndim))
        elif whole:
            in_specs.append(pl.BlockSpec(memory_space=pltpu.VMEM))
        else:
            in_specs.append(pl.BlockSpec(block, index))
    for shape, dtype, block, index in outs:
        if whole:
            out_specs.append(pl.BlockSpec(memory_space=pltpu.VMEM))
        else:
            out_specs.append(pl.BlockSpec(block, index))
        keep = whole and name != "final_stage"
        out_shape.append(
            pltpu.VMEM(shape, dtype) if keep else jax.ShapeDtypeStruct(shape, dtype)
        )
    return pl.pallas_call(
        kernel,
        grid=() if whole else (steps,),
        in_specs=in_specs,
        out_specs=out_specs,
        out_shape=out_shape,
        scratch_shapes=scratch,
        compiler_params=pltpu.CompilerParams(
            vmem_limit_bytes=(limit if whole else 56) * MIB
        ),
        cost_estimate=pl.CostEstimate(
            flops=flops // 1000, bytes_accessed=data // 1000, transcendentals=special // 1000
        ),
        name=name,
    )(*[value for value, _, _ in ins])


def fixed(value):
    return value, value.shape, lambda j: (0,) * value.ndim


def last(value, block):
    return value, value.shape[:-1] + (block,), lambda j: (0,) * (value.ndim - 1) + (j,)


def last_out(shape, dtype, block):
    return shape, dtype, shape[:-1] + (block,), lambda j: (0,) * (len(shape) - 1) + (j,)


def identity(size, order=lambda row: row):
    row = lax.broadcasted_iota(jnp.int32, (size, size), 0)
    column = lax.broadcasted_iota(jnp.int32, (size, size), 1)
    return (order(row) == column).astype(BF16)


def msa_kernel(msa_ref, cover_ref, left_w_ref, right_w_ref, right_ref, left_ref, values, rights, lefts):
    seqs, rows, breadth = msa_ref.shape
    proj = left_w_ref.shape[0]
    pairs = proj // 2
    tiles = breadth // LANES
    msa = msa_ref[...].astype(F32).reshape(seqs * rows, breadth)
    for tile in range(tiles):
        values[tile] = msa[:, tile * LANES : (tile + 1) * LANES]
    cover = cover_ref[...].astype(F32)
    swap = identity(proj, lambda row: 2 * (row % pairs) + row // pairs)
    right_w = jnp.dot(swap, right_w_ref[...], preferred_element_type=F32).astype(BF16)
    weights = jnp.concatenate([left_w_ref[...], right_w])
    for i in range(rows):
        row = jnp.concatenate(
            [values[tile, pl.ds(i, seqs, stride=rows), :] for tile in range(tiles)], axis=1
        )
        norm = standardize(row, -1).astype(BF16)
        factor = lax.dot_general(weights, norm, NT, preferred_element_type=F32)
        factor = factor * cover[i : i + 1]
        lefts[i] = factor[:proj]
        rights[i * pairs : (i + 1) * pairs] = jnp.concatenate(
            [factor[proj : proj + pairs], factor[proj + pairs :]], axis=1
        )
    half = rows // 2
    for i in range(half):
        left_ref[i * proj : (i + 1) * proj] = jnp.concatenate(
            [lefts[i], lefts[i + half]], axis=1
        ).astype(BF16)
    for t in range(pairs):
        right_ref[t] = rights[pl.ds(t, rows, stride=pairs), :].astype(BF16)
    right_ref[pairs] = jnp.concatenate([cover, jnp.zeros_like(cover)], axis=1).astype(BF16)


def msa_stage(msa, cover, left_w, right_w):
    seqs, rows, breadth = msa.shape
    proj = left_w.shape[0]
    right = (proj // 2 + 1, rows, 2 * seqs)
    left = (rows * proj // 2, 2 * seqs)
    return local_call(
        "msa_stage",
        msa_kernel,
        1,
        [fixed(msa), fixed(cover), fixed(left_w), fixed(right_w)],
        [(right, BF16, None, None), (left, BF16, None, None)],
        [
            pltpu.VMEM((breadth // LANES, seqs * rows, LANES), F32),
            pltpu.VMEM((rows * proj // 2, 2 * seqs), F32),
            pltpu.VMEM((rows, proj, seqs), F32),
        ],
        58,
        flops=4 * seqs * rows * breadth * proj,
        data=2 * seqs * rows * breadth,
        windows=True,
    )


def weights_kernel(
    mirror, out_ref, in_ref, gate_ref, final_ref, obs_ref, seen_ref, *refs
):
    out_t, in_t, gate_t, final_t, own_ref, far_ref, rows = refs
    one = identity(LANES)

    def turned(value):
        return lax.dot_general(one, value, NT, preferred_element_type=F32).astype(BF16)

    depth, width = out_ref.shape
    proj = int(depth**0.5)
    rows[...] = out_ref[...].astype(F32)
    ordered = jnp.concatenate([rows[pl.ds(q, proj, stride=proj), :] for q in range(proj)])
    out_t[...] = turned(ordered.astype(BF16))
    for k in range(in_ref.shape[1] // LANES):
        cols = slice(k * LANES, (k + 1) * LANES)
        in_t[cols] = turned(in_ref[:, cols])
    gate_t[...] = turned(gate_ref[...])
    final_t[...] = turned(final_ref[...])
    me = lax.axis_index("row")
    seen = seen_ref[...].astype(F32)
    for device, ref in ((me, own_ref), (mirror(me), far_ref)):
        for i in range(ref.shape[0]):
            ref[i : i + 1] = seen * obs_ref[device * ref.shape[0] + i].astype(F32)


def weights_stage(mirror, w_out, w_in, w_gate, w_final, obs, rows):
    depth, width = w_out.shape
    shapes = [w_out.shape[::-1], w_in.shape[::-1], w_gate.shape[::-1], w_final.shape[::-1]]
    return local_call(
        "weights_stage",
        lambda *refs: weights_kernel(mirror, *refs),
        1,
        [fixed(w_out), fixed(w_in), fixed(w_gate), fixed(w_final), scalars(obs)]
        + [fixed(obs[None])],
        [(shape, BF16, None, None) for shape in shapes]
        + [((rows,) + obs.shape, F32, None, None)] * 2,
        [pltpu.VMEM((depth, width), F32)],
        58,
        flops=2 * LANES * LANES * LANES * 6,
        data=4 * depth * width,
        windows=True,
    )


def order_right(right_refs, right):
    me = lax.axis_index("row")
    for index, ref in enumerate(right_refs):
        core, y = index // 2, index % 2
        for z in range(4):
            right[me ^ (4 * z + 2 * y + core)] = ref[z]


def make_updates(left_ref, mask, right, outer, scale):
    slices = right.shape[1]
    rows, depth, block = outer.shape
    proj = depth // (2 * (slices - 1))
    count = lax.dot_general(
        mask, right[:, slices - 1].reshape(block, LANES), NT, preferred_element_type=F32
    )
    scale[...] = 1.0 / jnp.maximum(count, 1.0)
    left = left_ref[...].astype(F32)
    turned = pltpu.roll(left, LANES // 2, 1)
    low = lax.broadcasted_iota(jnp.int32, left.shape, 1) < LANES // 2
    both_left = jnp.concatenate(
        [
            jnp.where(low, left, 0.0),
            jnp.where(low, turned, 0.0),
            jnp.where(low, 0.0, turned),
            jnp.where(low, 0.0, left),
        ]
    ).astype(BF16)
    half = rows * proj

    for t in range(slices - 1):
        both = lax.dot_general(
            both_left,
            right[:, t].reshape(block, LANES),
            NT,
            preferred_element_type=F32,
        ).astype(BF16)
        for e in range(2):
            outer[:, (2 * t + e) * proj : (2 * t + e + 1) * proj, :] = both[
                e * half : (e + 1) * half
            ].reshape(rows, proj, block)


def row_update(i, w_out_ref, outer, scale):
    update = jnp.dot(w_out_ref[...], outer[i], preferred_element_type=F32)
    return update * scale[i : i + 1]


def chip_here(split):
    return jnp.int32(0) if split == 1 else (lax.axis_index("row") // 2) & (split - 1)


def keep_sides(i, norm, w_in_ref, seen, sides_of, hidden):
    sides = jnp.dot(w_in_ref[...], norm, preferred_element_type=F32)
    stride = hidden + PAD
    for side, kept in enumerate(sides_of):
        gates = sides[2 * side * hidden : (2 * side + 1) * hidden]
        values = sides[(2 * side + 1) * hidden : (2 * side + 2) * hidden]
        value = sigmoid(gates) * values * seen
        for tile in range(kept.shape[0]):
            kept[tile, i * stride : i * stride + hidden] = value[
                :, tile * LANES : (tile + 1) * LANES
            ]


def write_sides(kept, outs, rows, hidden):
    per, chans = outs[0].shape[:2]
    chip = chip_here(len(outs))
    for part in range(per * len(outs)):
        target = outs[part // per].at[part % per]
        start = (chip ^ part) * chans

        @pl.loop(0, chans, unroll=8 if chans % 8 == 0 else chans)
        def _(c):
            for tile in range(kept.shape[0]):
                target[c, :, tile * LANES : (tile + 1) * LANES] = kept[
                    tile, pl.ds(start + c, rows, stride=hidden + PAD), :
                ].astype(BF16)


def pair_kernel(pieces, split, *refs):
    left_ref, mask_ref, couple_ref, w_out_ref, w_in_ref, seen_ref = refs[:6]
    right_refs, (pair_ref, *refs) = refs[6 : 6 + pieces], refs[6 + pieces :]
    a_refs, b_refs, refs = refs[:split], refs[split : 2 * split], refs[2 * split :]
    if pieces > 1:
        right, refs = refs[0], refs[1:]
        order_right(right_refs, right)
    else:
        right = right_refs[0]
    outer, kept_a, kept_b, scale = refs
    rows = couple_ref.shape[0]
    hidden = w_in_ref.shape[0] // 4
    make_updates(left_ref, mask_ref[...], right, outer, scale)
    for i in range(rows):
        pair = couple_ref[i].astype(F32).T + row_update(i, w_out_ref, outer, scale)
        norm = standardize(pair, 0).astype(BF16)
        pair_ref[i] = pair
        keep_sides(i, norm, w_in_ref, seen_ref[i : i + 1], (kept_a, kept_b), hidden)
    write_sides(kept_b, b_refs, rows, hidden)
    write_sides(kept_a, a_refs, rows, hidden)


def update_kernel(left_ref, w_out_ref, right, *refs):
    mask_refs, (update_ref, outer, scale) = refs[:-3], refs[-3:]
    if mask_refs:
        mask = mask_refs[0][...]
    else:
        mask = right[lax.axis_index("row") ^ 12, right.shape[1] - 1]
    make_updates(left_ref, mask, right, outer, scale)
    for i in range(update_ref.shape[0]):
        update_ref[i] = row_update(i, w_out_ref, outer, scale)


def mirror_kernel(update_ref, couple_ref, w_in_ref, seen_ref, *refs):
    outs, kept = refs[:-1], refs[-1]
    rows = couple_ref.shape[0]
    hidden = w_in_ref.shape[0] // 4
    for i in range(rows):
        pair = couple_ref[i].astype(F32).T + update_ref[i]
        norm = standardize(pair, 0).astype(BF16)
        keep_sides(i, norm, w_in_ref.at[2 * hidden :], seen_ref[i : i + 1], (kept,), hidden)
    write_sides(kept, outs, rows, hidden)


def right_input(value, total):
    return value, (value.shape[0] * BLOCK // total,) + value.shape[1:], lambda j: (j, 0, 0, 0)


def couple_input(couple):
    return couple, (couple.shape[0], BLOCK, couple.shape[2]), lambda j: (0, j, 0)


def kept_scratch(rows, hidden, block):
    return pltpu.VMEM((block // LANES, rows * (hidden + PAD), LANES), F32)


def scalars(value):
    return value, None, None


def pair_stage(left, right, mask, couple, w_out, w_in, seen, parts, split):
    rows, total, width = couple.shape
    hidden = w_in.shape[0] // 4
    piece = (parts // split, hidden // parts, rows, total)
    outs = [last_out((rows, width, total), F32, BLOCK)]
    outs += [last_out(piece, BF16, BLOCK)] * (2 * split)
    if len(right) > 1:
        outs += [((total // rows,) + right[0].shape[1:], BF16, None, None)]
    return local_call(
        "pair_stage",
        lambda *refs: pair_kernel(len(right), split, *refs),
        total // BLOCK,
        [fixed(left), fixed(mask), couple_input(couple), fixed(w_out), fixed(w_in)]
        + [last(seen, BLOCK)]
        + [right_input(value, total) for value in right],
        outs,
        [pltpu.VMEM((rows, w_out.shape[1], BLOCK), BF16)]
        + [kept_scratch(rows, hidden, BLOCK)] * 2
        + [pltpu.VMEM((rows, BLOCK), F32)],
        24,
        flops=4 * rows * total * w_out.shape[1] * width,
        data=16 * rows * total * width,
        special=2 * rows * total * hidden,
    )


def gate_kernel(pair_ref, w_gate_ref, gate_ref):
    for i in range(pair_ref.shape[0]):
        norm = standardize(pair_ref[i], 0).astype(BF16)
        gate_ref[i] = sigmoid(jnp.dot(w_gate_ref[...], norm, preferred_element_type=F32))


def gate_stage(pair, w_gate):
    rows, width, total = pair.shape
    return local_call(
        "gate_stage",
        gate_kernel,
        total // BLOCK,
        [last(pair, BLOCK), fixed(w_gate)],
        [last_out(pair.shape, F32, BLOCK)],
        [],
        16,
        flops=2 * rows * total * width * width,
        data=8 * rows * total * width,
        special=rows * total * width,
    )[0]


def update_stage(left, right, mask, w_out, rows, total):
    width = w_out.shape[0]
    return local_call(
        "update_stage",
        update_kernel,
        total // BLOCK,
        [fixed(left), fixed(w_out), right_input(right, total)]
        + ([] if mask is None else [fixed(mask)]),
        [last_out((rows, width, total), F32, BLOCK)],
        [pltpu.VMEM((rows, w_out.shape[1], BLOCK), BF16), pltpu.VMEM((rows, BLOCK), F32)],
        20,
        flops=4 * rows * total * w_out.shape[1] * width,
        data=8 * rows * total * width,
    )[0]


def mirror_stage(update, couple, w_in, seen, parts, split):
    rows, total, width = couple.shape
    hidden = w_in.shape[0] // 4
    return local_call(
        "mirror_stage",
        mirror_kernel,
        total // BLOCK,
        [last(update, BLOCK), couple_input(couple), fixed(w_in), last(seen, BLOCK)],
        [last_out((parts // split, hidden // parts, rows, total), BF16, BLOCK)] * split,
        [kept_scratch(rows, hidden, BLOCK)],
        16,
        flops=4 * rows * total * hidden * width,
        data=40000 * rows * total * width,
        special=rows * total * hidden,
    )


def tri_kernel(cores, split, flip, *refs):
    a_refs, refs = refs[:split], refs[split:]
    b_refs, refs = refs[: cores * split], refs[cores * split :]
    outs, whole = refs[:-1], refs[-1]
    per, chans, rows, total = a_refs[0].shape
    chip = chip_here(split)
    core = lax.axis_index("row") & 1
    for c in range(chans):
        for index, ref in enumerate(b_refs):
            for slot in range(per):
                part = (index % split) * per + slot
                place = (chip ^ part ^ flip) * cores
                if cores == 2:
                    place = place + (core ^ (index // split))
                whole[c, pl.ds(pl.multiple_of(place * rows, rows), rows), :] = ref[slot, c]
        side_a = jnp.concatenate([ref[slot, c] for ref in a_refs for slot in range(per)])
        product = lax.dot_general(side_a, whole[c], NT, preferred_element_type=F32).astype(BF16)
        for part in range(per * split):
            outs[part // per][part % per, c] = product[part * rows : (part + 1) * rows]


def channels(value, step):
    return value, value.shape[:1] + (step,) + value.shape[2:], lambda c: (0, c, 0, 0)


def tri_stage(a, b, cores, flip):
    split = len(a)
    per, chans, rows, total = a[0].shape
    step = max(1, min(chans, chans * BLOCK // total))
    half = per * split * cores * rows
    shape = (per, chans, rows, half)
    return local_call(
        "tri_stage",
        lambda *refs: tri_kernel(cores, split, flip, *refs),
        chans // step,
        [channels(value, step) for value in a]
        + [channels(value, step) for value in b],
        [(shape, BF16, (per, step, rows, half), lambda c: (0, c, 0, 0))] * split,
        [pltpu.VMEM((step, half, total), BF16)],
        16,
        flops=2 * chans * per * split * rows * half * total,
        data=6 * chans * half * total,
    )


def final_rows(tri, low, pair_ref, gate_ref, w_ref, normed, write):
    rows = pair_ref.shape[0]
    per, chans, _, block = tri[0].shape
    parts = per * len(tri)
    hidden = chans * parts
    tiles = block // LANES
    chip = chip_here(len(tri))
    values = standardize(
        jnp.concatenate([ref[slot] for ref in tri for slot in range(per)]).astype(F32), 0
    )
    for part in range(parts):
        first = pl.multiple_of((chip ^ part) * (chans * rows), chans * rows)
        for tile in range(tiles):
            normed[tile, pl.ds(first, chans * rows), :] = values[
                part * chans : (part + 1) * chans, :, tile * LANES : (tile + 1) * LANES
            ].reshape(chans * rows, LANES)
    for i in range(rows):
        columns = jnp.concatenate(
            [normed[tile, pl.ds(i, hidden, stride=rows), :] for tile in range(tiles)], axis=1
        ).astype(BF16)
        update = jnp.dot(w_ref[...], columns, preferred_element_type=F32)
        cols = pl.ds(low, block)
        result = pair_ref[i, :, cols] + gate_ref[i, :, cols] * update
        write(i, result.T.astype(BF16))


def half_start(far, block):
    mine = lax.div(lax.axis_index("row"), lax.axis_size("row") // 2)
    return pl.multiple_of((mine ^ far) * block, block)


def near_kernel(pair_ref, gate_ref, w_ref, *refs):
    tri, (out_ref, normed) = refs[:-2], refs[-2:]

    def write(i, result):
        out_ref[i] = result

    low = half_start(0, tri[0].shape[-1])
    final_rows(tri, low, pair_ref, gate_ref, w_ref, normed, write)


def near_stage(tri, pair, gate, weight):
    rows, width, _ = pair.shape
    hidden, block = weight.shape[1], tri[0].shape[-1]
    return local_call(
        "near_stage",
        near_kernel,
        1,
        [fixed(pair), fixed(gate), fixed(weight)] + [fixed(value) for value in tri],
        [((rows, block, width), BF16, None, None)],
        [pltpu.VMEM((block // LANES, hidden * rows, LANES), F32)],
        16,
        flops=2 * rows * block * hidden * width,
        data=12 * rows * block * width,
    )[0]


def final_kernel(split, pair_ref, gate_ref, w_ref, *refs):
    out_ref, normed = refs[-2:]
    tri, near = refs[:split], refs[split:-2]
    block = tri[0].shape[-1]
    low = half_start(1, block) if near else 0

    def write(i, result):
        out_ref[i, pl.ds(low, block), :] = result
        if near:
            out_ref[i, pl.ds(half_start(0, block), block), :] = near[0][i]

    final_rows(tri, low, pair_ref, gate_ref, w_ref, normed, write)


def final_stage(tri, near, pair, gate, weight):
    rows, width, total = pair.shape
    hidden, split = weight.shape[1], len(tri)
    block = BLOCK if near is None else tri[0].shape[-1]
    return local_call(
        "final_stage",
        lambda *refs: final_kernel(split, *refs),
        total // BLOCK,
        [last(pair, BLOCK), last(gate, BLOCK), fixed(weight)]
        + [last(value, block) for value in tri]
        + ([] if near is None else [fixed(near)]),
        [((rows, total, width), BF16, (rows, BLOCK, width), lambda j: (0, j, 0))],
        [pltpu.VMEM((block // LANES, hidden * rows, LANES), F32)],
        24,
        flops=2 * rows * total * hidden * width,
        data=12 * rows * total * width,
    )[0]


def send(value, move):
    devs = lax.axis_size("row")
    return lax.ppermute(value, "row", [(i, move(i)) for i in range(devs)])


def after(first, value):
    return lax.optimization_barrier((first, value))


def exchange(pieces, earlier=None):
    devs = lax.axis_size("row")
    half = devs // 2
    if len(pieces) == 1:
        groups = [list(range(half)), list(range(half, devs))]
        return [
            lax.all_to_all(
                pieces[0], "row", split_axis=0, concat_axis=0, tiled=True, axis_index_groups=groups
            )
        ]
    out = list(pieces)
    for r in range(1, len(out)):
        if earlier is not None:
            _, out[r] = after(earlier[r], out[r])
        out[r] = send(out[r], lambda i, r=r: i ^ (2 * r))
    return out


def with_other_core(pieces):
    if len(pieces) == 1:
        return pieces
    return list(pieces) + [send(value, lambda i: i ^ 1) for value in pieces]


def body(
    homolog_features,
    coverage_indicator,
    couple_features,
    observed_indicator,
    first_factor_matrix,
    second_factor_matrix,
    product_final_matrix,
    edge_projection_matrix,
    sigmoid_filter_matrix,
    multiplicative_final_matrix,
):
    rows, total, width = couple_features.shape
    devs = lax.axis_size("row")
    half = devs // 2
    me = lax.axis_index("row")
    hops = devs == 16
    cores = 2 if hops else 1
    parts = half // cores
    split = parts if hops else 1

    def mirror(device):
        return device ^ 12 if hops else (device + half) % devs

    def mirrored(value):
        return send(value, mirror)

    block, left = msa_stage(
        homolog_features,
        coverage_indicator.T,
        first_factor_matrix.T,
        second_factor_matrix.T,
    )
    weights = weights_stage(
        mirror,
        product_final_matrix,
        edge_projection_matrix,
        sigmoid_filter_matrix,
        multiplicative_final_matrix,
        observed_indicator,
        rows,
    )
    if hops:
        slices = block.shape[0]
        both = send(jnp.concatenate([block, left.reshape((-1,) + block.shape[1:])]), mirror)
        held = [block, send(block, lambda i: i ^ 4), send(block, lambda i: i ^ 8), both[:slices]]
        far_left = both[slices:].reshape(left.shape)
        held, (couple_out, weights) = after(jnp.stack(held), (couple_features, weights))
        far_couple = mirrored(couple_out)
        other = send(held, lambda i: i ^ 2)
        right = [held, other, send(held, lambda i: i ^ 1), send(other, lambda i: i ^ 1)]
        far_mask = None
    else:
        right = [lax.all_gather(block, "row", axis=0)]
        far_left = mirrored(left)
        far_couple = mirrored(couple_features)
        far_mask = right[0][mirror(me), -1]
    w_out, w_in, w_gate, w_final, seen, far_seen = weights

    pair, *sides = pair_stage(
        left, right, block[-1], couple_features, w_out, w_in, seen, parts, split
    )
    a, b = list(sides[:split]), list(sides[split : 2 * split])
    ordered = sides[2 * split] if hops else right[0]
    b = exchange(b)
    if hops:
        _, far_left = after(b[1], far_left)
    update = update_stage(far_left, ordered, far_mask, w_out, rows, total)
    if hops:
        update, a[2] = after(update, a[2])
    a = exchange(a, b)
    near = tri_stage(a, with_other_core(b), cores, 0)
    far_b = mirror_stage(update, far_couple, w_in, far_seen, parts, split)
    if hops:
        far_b = list(far_b)
        _, far_b[1] = after(a[3], far_b[1])
        _, far_b[2:] = after(a[1], far_b[2:])
    far_b = exchange(far_b)
    if hops:
        _, pair = after(far_b[1], pair)
    gate = gate_stage(pair, w_gate)
    if hops:
        near, far_b = after(near, far_b)
    near = exchange(near)
    far = exchange(tri_stage(a, with_other_core(far_b), cores, 2 if hops else 0))
    if hops:
        done = near_stage(near, pair, gate, w_final)
        return final_stage(far, done, pair, gate, w_final)
    lower = me < half
    tri = [
        jnp.concatenate([jnp.where(lower, x, y), jnp.where(lower, y, x)], axis=-1)
        for x, y in zip(near, far)
    ]
    return final_stage(tri, None, pair, gate, w_final)


def solution(mesh):
    placed = (
        P(None, ("groups", "row"), None),
        P(None, ("groups", "row")),
        P(("groups", "row"), None, None),
        P("groups"),
        P(),
        P(),
        P(),
        P(),
        P(),
        P(),
    )
    return jax.shard_map(
        body,
        mesh=mesh,
        in_specs=placed,
        out_specs=P(("groups", "row"), None, None),
        check_vma=False,
    )
```
